512 devices in a mesh: sect: 32 (over z, y_lo), tp: 16 (over y_hi, x, core).
Axes of the slice: x: 4, y: 4 (y_hi: 2, y_lo: 2; y = y_hi * 2 + y_lo), z: 16, core: 2. Of those that a mesh axis runs over, the one named last changes fastest.
Arguments:
- hidden_pre: bfloat16 [16384, 8192], P('sect', 'tp'), may hold values from -30 to 30
- norm_gain: bfloat16 [8192], P('tp'), may hold values from 0.099609375 to 1.8984375
- kv_weight: bfloat16 [8192, 2048], P('tp'), may hold values from -0.0625 to 0.0625
- query_pre: bfloat16 [16384, 8192], P('sect', 'tp'), may hold values from -600 to 600
- doc_ids: int32 [32, 512], P('sect'), may hold values from 0 to 7, never falling along the last dimension, each value on 1 to 256 neighbouring positions
- page_dest: int32 [1024, 1], P('sect'), may hold values from 0 to 31, as said below
- old_pages: bfloat16 [512, 16, 16, 128], P('sect'), may hold values from -6 to 6
- query_dec: bfloat16 [512, 8192], P('sect', 'tp'), may hold values from -600 to 600
- page_table: int32 [512, 16], P('sect'), may hold values from 0 to 79, as said below
- ctx_len: int32 [512], P('sect'), may hold values from 1 to 256, as said below
Outputs:
- prefill_out: bfloat16 [16384, 8192], P('sect', 'tp')
- decode_out: bfloat16 [512, 8192], P('sect', 'tp')
The draws below stay inside these ranges and needn't reach their ends.
Inputs may be any that keep to these rules, and one draw needn't show every extreme that they name: `page_dest`: of one section's pages at most 2 go to any one section, and in every section's pages some section receives exactly 2. `page_table`: the entries of a row are distinct; each names a slot below 16 or a slot 16 + s * 2 + c of the row's own section where c is below the number of pages that section s hands to it. `ctx_len`: in every section some row has the full context of 256 tokens.
All inputs are finite; a program needn't handle non-finite values.
Results may differ from the reference program's by a relative error of at most 0.012.
The reference program's roundings to bfloat16 on the way count: a program that leaves them out, or rounds other values in their place, can miss the bound.
Values may be sent and summed in bfloat16 or wider, within the bound.
A program may use at most 64 MiB of HBM per device.

```python
import math
import jax
import jax.numpy as jnp
import numpy as np
from jax import lax

D = 8192
HEADS = 64
KVH = 8
HD = 128
PAGE = 16
MAXP = 16
DOCS = 8
PTOK_DEV = 512
ROWS_DEV = 16
OLD_PAGES = 16
PAGES_DEV = 32
CAP = 2
POOL = 80
PTOK = 16384
ROWS = 512
N_SECT = 32


def scaled_queries(key, row_total, col_total, top_scale):
    key_values, key_scale = jax.random.split(key)
    row_scale = jnp.exp(jax.random.uniform(key_scale, (row_total, 1), jnp.float32, 0.0, math.log(top_scale)))
    values = jax.random.normal(key_values, (row_total, col_total), jnp.float32) * row_scale
    return jnp.clip(values, -6.0 * row_scale, 6.0 * row_scale).astype(jnp.bfloat16)


def placement_table(key):
    key_noise, key_favour, key_popular = jax.random.split(key, 3)
    slot_total = N_SECT * CAP
    slot_index = jnp.arange(slot_total, dtype=jnp.int32)
    slot_holder = slot_index // CAP
    jitter_noise = jax.random.randint(key_noise, (N_SECT, slot_total), 0, 2 ** 16)
    preferred_slots = jax.random.randint(key_favour, (N_SECT, 1), 0, N_SECT)
    frequent_pages = jax.random.randint(key_popular, (N_SECT,), 0, 4) == 0
    extra_score = jnp.where(slot_holder[None, :] == preferred_slots, 2 ** 18, 0) + jnp.where(frequent_pages[slot_holder], 2 ** 17, 0)[None, :]
    sorted_ranking = (jitter_noise + extra_score) * 2048 + slot_index[None, :]
    chosen = lax.top_k(sorted_ranking, PAGES_DEV)[1]
    return (chosen // CAP).astype(jnp.int32)


def draw_hidden_pre(key, part):
    key = jax.random.fold_in(key, 11)
    key_base = jax.random.fold_in(key, 0)
    columns = jnp.sqrt(1.0 + 2.0 * jnp.arange(D, dtype=jnp.float32) / D)[None, :]
    values = jax.random.normal(key_base, (PTOK, D), jnp.float32) * columns
    return jnp.clip(values, -30.0, 30.0).astype(jnp.bfloat16)


def draw_query_pre(key, part):
    key = jax.random.fold_in(key, 13)
    return scaled_queries(key, PTOK, HEADS * HD, 1.0)


def draw_query_dec(key, part):
    key = jax.random.fold_in(key, 17)
    return scaled_queries(key, ROWS, HEADS * HD, 1.0)


def draw_page_dest(key, part):
    targets = placement_table(key)
    return targets.reshape(N_SECT * PAGES_DEV, 1)


def draw_page_table(key, part):
    targets = placement_table(key)
    key = jax.random.fold_in(key, 23)
    sent = jnp.sum(targets[:, :, None] == jnp.arange(N_SECT)[None, None, :], axis=1)
    rank_ids = jnp.arange(CAP)
    filled = rank_ids[None, None, :] < sent.T[:, :, None]
    usable = jnp.concatenate([jnp.ones((N_SECT, OLD_PAGES), jnp.bool_), filled.reshape(N_SECT, N_SECT * CAP)], axis=1)
    jitter_noise = jax.random.randint(key, (N_SECT, ROWS_DEV, POOL), 1, 2 ** 16)
    sorted_ranking = jnp.where(usable[:, None, :], jitter_noise, 0) * 4096 + jnp.arange(POOL)[None, None, :]
    chosen = lax.top_k(sorted_ranking, MAXP)[1]
    return chosen.reshape(N_SECT * ROWS_DEV, MAXP).astype(jnp.int32)


def draw_ctx_len(key, part):
    key = jax.random.fold_in(key, 31)
    lengths = jax.random.randint(key, (N_SECT, ROWS_DEV), 1, MAXP * PAGE + 1)
    lengths = lengths.at[:, 0].set(MAXP * PAGE)
    return lengths.reshape(N_SECT * ROWS_DEV).astype(jnp.int32)


def block_scale(key, dims, pieces, smallest, largest):
    def one(position, parts):
        draws = jax.random.uniform(jax.random.fold_in(jax.random.fold_in(key, 6), position), (parts,), jnp.float32, smallest / len(pieces), largest / len(pieces))
        return jnp.repeat(jnp.exp(draws), dims[position] // parts).reshape((-1,) + (1,) * (len(dims) - position - 1))

    loudness = one(*pieces[0])
    for cut in pieces[1:]:
        loudness = loudness * one(*cut)
    return loudness


def profile(number_of, total, reach, skew):
    weights = [(1 << 20) // math.isqrt(standing ** skew) + 1 for standing in range(2, number_of + 1)]
    surplus, holding = total - reach - (number_of - 1), [1] * (number_of - 1)
    while surplus > 0:
        free = [i for i in range(number_of - 1) if holding[i] < reach]
        mass, left = sum([weights[i] for i in free]), surplus
        for i in free:
            addition = min(reach - holding[i], max(1, left * weights[i] // mass), surplus)
            holding[i] = holding[i] + addition
            surplus = surplus - addition
    return np.array([reach] + holding)


def uneven(rng, amount, total, bound, slope):
    if amount == 2:
        one = jax.random.randint(rng, (), max(1, total - bound), min(bound, total - 1) + 1)
        return jnp.stack([one, total - one])
    tallies = jnp.asarray(profile(amount, total, bound, slope), jnp.int32)
    twos = (amount - 1) // 2
    source_of, sink = tallies[1:1 + 2 * twos:2], tallies[2:2 + 2 * twos:2]
    margin = jnp.minimum(source_of - 1, bound - sink)
    shifted = jax.random.randint(jax.random.fold_in(rng, 1), (twos,), 0, 1 << 20) % (margin + 1)
    tallies = tallies.at[1:1 + 2 * twos:2].set(source_of - shifted).at[2:2 + 2 * twos:2].set(sink + shifted)
    return tallies[jax.random.permutation(jax.random.fold_in(rng, 2), amount)]


def bell_draw(own_key, shape, deviation, bound, cuts=(), kind=jnp.bfloat16):
    loudness = block_scale(own_key, shape, cuts, -0.22, 0.18) if cuts else 1.0
    array = jax.random.normal(own_key, shape, jnp.float32) * deviation * loudness
    return jnp.minimum(jnp.maximum(array, -bound), bound).astype(kind)


def setup_inputs(seed: int = 0) -> dict:
    key_list = jax.random.split(jax.random.key(seed), 11)
    hidden_pre = draw_hidden_pre(jax.random.fold_in(key_list[10], 71), 0)
    norm_gain = jnp.clip(1.0 + 0.18 * jax.random.normal(key_list[1], (D,), jnp.float32), 0.099609375, 1.8984375).astype(jnp.bfloat16)
    kv_weight = bell_draw(key_list[2], (D, 2 * KVH * HD), D ** -0.5, 0.0625, ((0, 16),))
    query_pre = draw_query_pre(jax.random.fold_in(key_list[10], 71), 0)
    doc_ids = jax.vmap(lambda own: jnp.searchsorted(jnp.cumsum(uneven(own, DOCS, PTOK_DEV, PTOK_DEV // 2, 1)), jnp.arange(PTOK_DEV), side="right"))(jax.random.split(key_list[4], N_SECT)).reshape((N_SECT, PTOK_DEV)).astype(jnp.int32)
    page_dest = draw_page_dest(jax.random.fold_in(key_list[10], 71), 0)
    old_pages = bell_draw(key_list[6], (N_SECT * OLD_PAGES, PAGE, 2 * KVH, HD), 1.0, 6.0, ((0, 32),))
    query_dec = draw_query_dec(jax.random.fold_in(key_list[10], 71), 0)
    page_table = draw_page_table(jax.random.fold_in(key_list[10], 71), 0)
    ctx_len = draw_ctx_len(jax.random.fold_in(key_list[10], 71), 0)
    return {"hidden_pre": hidden_pre, "norm_gain": norm_gain, "kv_weight": kv_weight, "query_pre": query_pre, "doc_ids": doc_ids, "page_dest": page_dest, "old_pages": old_pages, "query_dec": query_dec, "page_table": page_table, "ctx_len": ctx_len}


NORM_EPS = 1e-05

def softmax_rows(scores):
    row_peak = lax.optimization_barrier(jnp.max(scores, axis=-1, keepdims=True))
    raised = jnp.exp(scores - row_peak)
    return raised / lax.optimization_barrier(jnp.sum(raised, axis=-1, keepdims=True))

def rounded_operand(weights):
    narrow = lax.optimization_barrier(weights.astype(jnp.bfloat16))
    return narrow.astype(jnp.float32)

def reference(hidden_pre, norm_gain, kv_weight, query_pre, doc_ids, page_dest, old_pages, query_dec, page_table, ctx_len):
    widened = hidden_pre.astype(jnp.float32)
    mean_square = lax.optimization_barrier(jnp.mean(widened * widened, axis=1, keepdims=True))
    scaled = (widened * norm_gain.astype(jnp.float32)).astype(jnp.bfloat16)
    projected = jnp.dot(scaled, kv_weight, preferred_element_type=jnp.float32)
    kv_all = (projected * lax.rsqrt(mean_square + NORM_EPS)).astype(jnp.bfloat16)
    kv_split = kv_all.reshape(N_SECT, PTOK_DEV, KVH, 2, HD)
    prompt_queries = query_pre.reshape(N_SECT, PTOK_DEV, KVH, HEADS // KVH, HD)
    factor = HD ** (-0.5)
    positions = jnp.arange(PTOK_DEV)

    def prefill_section(items):
        queries, kv_pairs, doc_row = items
        scores = jnp.einsum('tgnd,sgd->gnts', queries.astype(jnp.float32), kv_pairs[:, :, 0].astype(jnp.float32)) * factor
        allowed = (doc_row[:, None] == doc_row[None, :]) & (positions[None, :] <= positions[:, None])
        scores = jnp.where(allowed, scores, -jnp.inf)
        weights = rounded_operand(softmax_rows(scores))
        mixed = jnp.einsum('gnts,sgd->tgnd', weights, kv_pairs[:, :, 1].astype(jnp.float32))
        return mixed.reshape(PTOK_DEV, HEADS * HD).astype(jnp.bfloat16)
    prefill_out = lax.map(prefill_section, (prompt_queries, kv_split, doc_ids)).reshape(PTOK, HEADS * HD)
    targets_by_sect = page_dest[:, 0].reshape(N_SECT, PAGES_DEV)
    page_order = jnp.arange(PAGES_DEV)
    earlier = (targets_by_sect[:, None, :] == targets_by_sect[:, :, None]) & (page_order[None, None, :] < page_order[None, :, None])
    rank_within = lax.optimization_barrier(jnp.sum(earlier, axis=2)).astype(jnp.int32)
    source = jnp.arange(N_SECT, dtype=jnp.int32)[:, None]
    target = targets_by_sect * (N_SECT * CAP) + source * CAP + rank_within
    page_ids = jnp.arange(N_SECT * PAGES_DEV, dtype=jnp.int32)
    page_owner = jnp.full((N_SECT * N_SECT * CAP,), -1, jnp.int32).at[target.reshape(-1)].set(page_ids)
    page_owner = page_owner.reshape(N_SECT, N_SECT * CAP)
    kv_pages = kv_all.reshape(N_SECT * PAGES_DEV, PAGE, 2 * KVH * HD)
    resident = old_pages.reshape(N_SECT, OLD_PAGES, PAGE, 2 * KVH * HD)
    decode_queries = query_dec.reshape(N_SECT, ROWS_DEV, KVH, HEADS // KVH, HD)
    tables = page_table.reshape(N_SECT, ROWS_DEV, MAXP)
    lengths = ctx_len.reshape(N_SECT, ROWS_DEV)
    ctx_count = MAXP * PAGE
    ctx_positions = jnp.arange(ctx_count)

    def decode_section(items):
        queries, table_rows, length_rows, old_rows, owners = items
        fresh = kv_pages[jnp.maximum(owners, 0)]
        fresh = jnp.where((owners >= 0)[:, None, None], fresh, jnp.zeros_like(fresh))
        page_pool = jnp.concatenate([old_rows, fresh], axis=0)
        picked = page_pool[table_rows].reshape(ROWS_DEV, ctx_count, KVH, 2, HD).astype(jnp.float32)
        scores = jnp.einsum('rgnd,rcgd->rgnc', queries.astype(jnp.float32), picked[:, :, :, 0]) * factor
        live_mask = ctx_positions[None, :] < length_rows[:, None]
        scores = jnp.where(live_mask[:, None, None, :], scores, -jnp.inf)
        weights = rounded_operand(softmax_rows(scores))
        mixed = jnp.einsum('rgnc,rcgd->rgnd', weights, picked[:, :, :, 1])
        return mixed.reshape(ROWS_DEV, HEADS * HD).astype(jnp.bfloat16)
    decode_out = lax.map(decode_section, (decode_queries, tables, lengths, resident, page_owner)).reshape(ROWS, HEADS * HD)
    return (prefill_out, decode_out)
```

```python
import jax
import jax.numpy as jnp
from jax import lax
from jax.sharding import PartitionSpec as P
import jax.experimental.pallas as pl
import jax.experimental.pallas.tpu as pltpu

D = 8192
HD = 128
PAGE = 16
TOK = 512
FEAT = 512
CHIPS = 8
SECT = 32
SLOTS = 2
MSG = SLOTS * PAGE
FRESH = SECT * MSG
ROWS = 16
NH = 4
OLD = 256
MAXP = 16
NORM_EPS = 1e-05
SCALE = HD ** -0.5
MESH = pl.DeviceIdType.MESH
F32 = jnp.float32
BF16 = jnp.bfloat16
RING = ((1, 2), (1, 1), (1, 3), (0, 2), (1, 0), (0, 1), (0, 3))
NEG = -jnp.inf
TINY = 1e-30
STEPS = 32000.0
VMEM_LIMIT = 60 * 2**20


def dot(a, b):
    return lax.dot_general(a, b, (((1,), (0,)), ((), ())), preferred_element_type=F32)


def dot_t(a, b):
    return lax.dot_general(a, b, (((1,), (1,)), ((), ())), preferred_element_type=F32)


def softmax_weights(scores):
    peak = jnp.max(scores, axis=-1, keepdims=True)
    raised = jnp.exp(scores - peak)
    return (raised * (1.0 / jnp.sum(raised, axis=-1, keepdims=True))).astype(BF16)


def kernel(
    hid, gain, weight, qpre, doc, pdest, oldp, qdec, table, ctx,
    o_pre, o_dec,
    hraw, graw, wv, docv, pdv, tabv, ctxs, hs, st, part, sibp, sbuf, rs, sstat, rstat, chooser, outg, kvh, pool,
    oldbuf, oldkv, qp, qd, pos, obuf, dbuf,
    in_sem, w_sem, sib_s, sib_r, ps_s, ps_r, rs_s, rs_r, sq_s, sq_r, aa_s, aa_r, out_sem, flood,
):
    s = lax.axis_index("sect")
    t = lax.axis_index("tp")
    k = t % 2
    x = (t // 2) % 4
    yh = t // 8
    g = t // 2
    z = s // 2
    yl = s % 2
    sib = (s, t + 1 - 2 * k)

    def ring_dst(i):
        dy, dx = RING[i]
        return ((yh + dy) % 2) * 4 + (x + dx) % 4

    def ring_src(i):
        dy, dx = RING[i]
        return ((yh + dy) % 2) * 4 + (x + 4 - dx) % 4

    def sect_peer(i):
        j = i // 2
        sign = 1 - 2 * (j % 2)
        dz = 8 + sign * ((j + 1) // 2)
        yx = 1 - i % 2
        return dz, yx

    def z_peer(dz, yx):
        return (((z + dz + 16) % 16) * 2 + (yl + yx) % 2, t)

    def remote(src, dst, ss, rr, dev):
        c = pltpu.make_async_remote_copy(
            src_ref=src, dst_ref=dst, send_sem=ss, recv_sem=rr, device_id=dev, device_id_type=MESH
        )
        c.start()
        return c

    def load(src, dst, sem):
        c = pltpu.make_async_copy(src, dst, sem)
        c.start()
        return c

    bar = pltpu.get_barrier_semaphore()
    greeted = [sib] + [(s, ring_dst(i) * 2 + k) for i in range(7)]
    greeted += [z_peer(1, 0), z_peer(-1, 0), z_peer(1, 1), z_peer(-1, 1), z_peer(0, 1)]
    for peer in greeted:
        pl.semaphore_signal(bar, inc=1, device_id=peer, device_id_type=MESH)

    order = [ring_dst(i) for i in range(7)] + [g]
    c_hid = load(hid, hraw, in_sem.at[0])
    c_gain = load(gain, graw, in_sem.at[1])
    c_w = [
        load(
            weight.at[:, pl.ds(pl.multiple_of(j * 2 * HD, 2 * HD), 2 * HD)], wv.at[j], w_sem.at[n]
        )
        for n, j in enumerate(order)
    ]
    c_pd = load(pdest, pdv, in_sem.at[2])
    c_doc = load(doc, docv, in_sem.at[3])
    c_tab = load(table, tabv, in_sem.at[4])
    c_ctx = load(ctx, ctxs, in_sem.at[5])
    c_old = load(oldp, oldbuf, in_sem.at[6])
    c_qp = load(qpre, qp, in_sem.at[7])
    c_qd = load(qdec, qd, in_sem.at[8])

    c_hid.wait()
    c_gain.wait()
    h = hraw[...].astype(F32)
    hs[...] = (h * graw[...].astype(F32).reshape(1, FEAT)).astype(BF16)
    hh = h * h
    folded = hh[:, 0:128] + hh[:, 128:256] + hh[:, 256:384] + hh[:, 384:512]
    st[k] = jnp.broadcast_to(jnp.sum(folded.T, axis=0, keepdims=True), (8, TOK))
    for n, j in enumerate(order):
        c_w[n].wait()
        both = dot(hs[...], wv[j])
        part[j, 0] = both[:, :HD]
        part[j, 1] = both[:, HD:]

    pl.semaphore_wait(bar, len(greeted))

    c_st = remote(st.at[k], st.at[k], sib_s.at[0], sib_r.at[0], sib)
    c_ps = [
        remote(part.at[j, 1 - k], sibp.at[j], ps_s.at[n], ps_r.at[n], sib) for n, j in enumerate(order)
    ]
    c_st.wait_recv()
    chip_sq = st[0] + st[1]
    chip_ms = chip_sq * (1.0 / (2 * FEAT)) + TINY
    row_mul = lax.rsqrt(chip_ms).T[:, 0:1]
    sstat[g, :, 0:TOK] = chip_sq
    c_rs, c_sq = [], []
    for n, j in enumerate(order):
        c_ps[n].wait_recv()
        total = part[j, k] + sibp[j]
        if n < 7:
            level = total * row_mul
            top = jnp.maximum(jnp.max(jnp.abs(level), axis=0, keepdims=True), TINY)
            sbuf[j] = jnp.round(level * (STEPS / top)).astype(jnp.int32).astype(jnp.int16)
            sstat[j, :, 0:TOK] = chip_sq
            sstat[j, :, TOK:] = jnp.broadcast_to(top * (1.0 / STEPS), (8, HD))
            peer = (s, j * 2 + k)
            c_sq.append(remote(sstat.at[j], rstat.at[g], sq_s.at[n], sq_r.at[n], peer))
            c_rs.append(remote(sbuf.at[j], rs.at[g], rs_s.at[n], rs_r.at[n], peer))
        else:
            part[j, k] = total

    def flood_round(r):
        for sign in (1, -1):
            pl.semaphore_signal(
                flood.at[r], inc=1, device_id=z_peer(sign * (1 << r), 0), device_id_type=MESH
            )
        pl.semaphore_wait(flood.at[r], 2)

    flood_round(0)

    c_pd.wait()
    eye = lax.broadcasted_iota(jnp.int32, (32, 32), 0) == lax.broadcasted_iota(jnp.int32, (32, 32), 1)
    page_col = jnp.sum(jnp.where(eye, jnp.broadcast_to(pdv[...], (32, 32)), 0), axis=1, keepdims=True)
    page_of = lax.broadcasted_iota(jnp.int32, (32, TOK), 1) // PAGE
    page_row = lax.broadcasted_iota(jnp.int32, (32, TOK), 0)
    page_b = jnp.broadcast_to(page_col, (32, TOK))
    dest_tok = jnp.sum(jnp.where(page_of == page_row, page_b, 0), axis=0, keepdims=True)
    rank_tok = jnp.sum(
        jnp.where((page_b == dest_tok) & (page_row < page_of), 1, 0), axis=0, keepdims=True
    )
    tok_in = lax.broadcasted_iota(jnp.int32, (1, TOK), 1) % PAGE
    target = (dest_tok * SLOTS + rank_tok) * PAGE + tok_in
    for c in range(FRESH // 128):
        rows = lax.broadcasted_iota(jnp.int32, (128, TOK), 0) + c * 128
        chooser[c * 128:(c + 1) * 128, :] = jnp.where(rows == target, 1.0, 0.0).astype(BF16)

    flood_round(1)

    c_old.wait()
    for c in range(OLD // 32):
        blk = oldbuf[2 * c:2 * c + 2].reshape(32, 16, HD).astype(F32)
        head = lax.broadcasted_iota(jnp.int32, (1, 16, 1), 1)
        for m in range(2):
            one = jnp.sum(jnp.where(head == 2 * g + m, blk, 0.0), axis=1)
            oldkv[m, c * 32:(c + 1) * 32, :] = one.astype(BF16)

    c_tab.wait()
    c_ctx.wait()
    col = lax.broadcasted_iota(jnp.int32, (ROWS, OLD + FRESH), 1)
    col_slot = col // PAGE
    col_in = col % PAGE
    where_pos = jnp.full((ROWS, OLD + FRESH), 1 << 20, jnp.int32)
    tab = tabv[...]
    for j in range(MAXP):
        where_pos = jnp.where(tab[:, j:j + 1] == col_slot, j * PAGE + col_in, where_pos)
    row_id = lax.broadcasted_iota(jnp.int32, (ROWS, 1), 0)
    lens = jnp.zeros((ROWS, 1), jnp.int32)
    for r in range(ROWS):
        lens = jnp.where(row_id == r, ctxs[r], lens)
    pos[...] = jnp.where(where_pos < lens, 0.0, NEG)

    flood_round(2)

    summed = part[g, k]
    total_sq = chip_sq
    for i in (5, 6, 3, 4, 1, 2, 0):
        c_sq[i].wait_recv()
        src = ring_src(i)
        other_sq = rstat[src, :, 0:TOK]
        total_sq = total_sq + other_sq
        other_ms = other_sq * (1.0 / (2 * FEAT)) + TINY
        row_scale = (other_ms * lax.rsqrt(other_ms)).T[:, 0:1]
        col_scale = rstat[src, 0:1, TOK:]
        c_rs[i].wait_recv()
        summed = summed + rs[src].astype(jnp.int32).astype(F32) * col_scale * row_scale
    inv = lax.rsqrt(total_sq / D + NORM_EPS).T[:, 0:1]
    kvh[k] = (summed * inv).astype(BF16)
    c_kv = remote(kvh.at[k], kvh.at[k], sib_s.at[1], sib_r.at[1], sib)

    for c in range(4):
        outg[c * 256:(c + 1) * 256, :] = dot(chooser[c * 256:(c + 1) * 256, :], kvh[k]).astype(BF16)

    def page_copy(i):
        dz, yx = sect_peer(i)
        dst = ((z + dz) % 16) * 2 + (yl + yx) % 2
        return pltpu.make_async_remote_copy(
            src_ref=outg.at[pl.ds(pl.multiple_of(dst * MSG, MSG), MSG)],
            dst_ref=pool.at[k, pl.ds(pl.multiple_of(s * MSG, MSG), MSG)],
            send_sem=aa_s.at[i], recv_sem=aa_r.at[i], device_id=(dst, t), device_id_type=MESH,
        )

    def page_start(i, _):
        page_copy(i).start()
        return 0

    lax.fori_loop(0, 31, page_start, 0)
    own = pl.ds(pl.multiple_of(s * MSG, MSG), MSG)
    pool[k, own, :] = outg[own, :]

    c_qp.wait()
    c_doc.wait()
    doc_row = docv[...].astype(F32)
    doc_col = jnp.broadcast_to(doc_row, (8, TOK)).T[:, 0:1]
    c_kv.wait_recv()
    out_copies = []
    for b in range(4):
        lo, hi = max(0, b - 2) * 128, (b + 1) * 128
        q0 = b * 128
        tq = lax.broadcasted_iota(jnp.int32, (128, hi - lo), 0) + q0
        tk = lax.broadcasted_iota(jnp.int32, (128, hi - lo), 1) + lo
        allowed = (doc_col[q0:hi, :] == doc_row[:, lo:hi]) & (tk <= tq)
        keys = kvh[0, lo:hi, :]
        values = kvh[1, lo:hi, :]
        for n in range(NH):
            sc = dot_t(qp[q0:hi, n * HD:(n + 1) * HD], keys) * SCALE
            wts = softmax_weights(jnp.where(allowed, sc, NEG))
            obuf[q0:hi, n * HD:(n + 1) * HD] = dot(wts, values).astype(BF16)
        out_copies.append(load(obuf.at[q0:hi], o_pre.at[q0:hi], out_sem.at[b]))

    c_qd.wait()
    qs = jnp.concatenate([qd[:, n * HD:(n + 1) * HD] for n in range(NH)], axis=0)
    sc_old = dot_t(qs, oldkv[0]) * SCALE
    mask = pos[...]
    mask = jnp.concatenate([mask] * NH, axis=0)
    sc_old = sc_old + mask[:, :OLD]
    peak_old = jnp.max(sc_old, axis=-1, keepdims=True)

    def page_wait(i, _):
        page_copy(i).wait_recv()
        return 0

    lax.fori_loop(0, 31, page_wait, 0)
    c_pool = remote(pool.at[k], pool.at[k], sib_s.at[2], sib_r.at[2], sib)
    c_pool.wait_recv()
    sc_new = dot_t(qs, pool[0]) * SCALE + mask[:, OLD:]
    peak = jnp.maximum(peak_old, jnp.max(sc_new, axis=-1, keepdims=True))
    e_old = jnp.exp(sc_old - peak)
    e_new = jnp.exp(sc_new - peak)
    norm = 1.0 / (jnp.sum(e_old, axis=-1, keepdims=True) + jnp.sum(e_new, axis=-1, keepdims=True))
    mixed = dot((e_old * norm).astype(BF16), oldkv[1]) + dot((e_new * norm).astype(BF16), pool[1])
    mixed = mixed.astype(BF16)
    for n in range(NH):
        dbuf[:, n * HD:(n + 1) * HD] = mixed[n * ROWS:(n + 1) * ROWS]
    out_copies.append(load(dbuf, o_dec, out_sem.at[4]))

    for c in [c_st, c_kv, c_pool] + c_ps + c_rs + c_sq:
        c.wait_send()

    def page_sent(i, _):
        page_copy(i).wait_send()
        return 0

    lax.fori_loop(0, 31, page_sent, 0)
    for c in out_copies:
        c.wait()


def local(hidden_pre, norm_gain, kv_weight, query_pre, doc_ids, page_dest, old_pages, query_dec, page_table, ctx_len):
    any_spec = pl.BlockSpec(memory_space=pl.ANY)
    dma = pltpu.SemaphoreType.DMA
    vm = pltpu.VMEM
    I32 = jnp.int32
    return pl.pallas_call(
        kernel,
        name="serve",
        out_shape=(
            jax.ShapeDtypeStruct((TOK, NH * HD), BF16),
            jax.ShapeDtypeStruct((ROWS, NH * HD), BF16),
        ),
        in_specs=[any_spec] * 10,
        out_specs=(any_spec, any_spec),
        scratch_shapes=[
            vm((TOK, FEAT), BF16), vm((FEAT,), BF16), vm((CHIPS, FEAT, 2 * HD), BF16),
            vm((1, TOK), I32), vm((1, 32), I32), vm((ROWS, MAXP), I32), pltpu.SMEM((ROWS,), I32),
            vm((TOK, FEAT), BF16), vm((2, 8, TOK), F32),
            vm((CHIPS, 2, TOK, HD), F32), vm((CHIPS, TOK, HD), F32),
            vm((CHIPS, TOK, HD), jnp.int16), vm((CHIPS, TOK, HD), jnp.int16),
            vm((CHIPS, 8, TOK + HD), F32), vm((CHIPS, 8, TOK + HD), F32),
            vm((FRESH, TOK), BF16), vm((FRESH, HD), BF16), vm((2, TOK, HD), BF16), vm((2, FRESH, HD), BF16),
            vm((16, 16, 16, HD), BF16), vm((2, OLD, HD), BF16), vm((TOK, NH * HD), BF16),
            vm((ROWS, NH * HD), BF16), vm((ROWS, OLD + FRESH), F32),
            vm((TOK, NH * HD), BF16), vm((ROWS, NH * HD), BF16),
            dma((9,)), dma((8,)), dma((3,)), dma((3,)), dma((8,)), dma((8,)), dma((7,)), dma((7,)),
            dma((7,)), dma((7,)), dma((31,)), dma((31,)), dma((5,)), pltpu.SemaphoreType.REGULAR((3,)),
        ],
        compiler_params=pltpu.CompilerParams(
            collective_id=0, has_side_effects=True, vmem_limit_bytes=VMEM_LIMIT
        ),
    )(
        hidden_pre, norm_gain, kv_weight, query_pre, doc_ids, page_dest.reshape(1, 32), old_pages,
        query_dec, page_table, ctx_len,
    )


def solution(mesh):
    in_specs = (
        P("sect", "tp"),
        P("tp"),
        P("tp", None),
        P("sect", "tp"),
        P("sect", None),
        P("sect", None),
        P("sect", None, None, None),
        P("sect", "tp"),
        P("sect", None),
        P("sect"),
    )
    out_specs = (P("sect", "tp"), P("sect", "tp"))
    return jax.shard_map(local, mesh=mesh, in_specs=in_specs, out_specs=out_specs, check_vma=False)
```

```python
import jax
import jax.numpy as jnp
from jax import lax
from jax.sharding import PartitionSpec as P
import jax.experimental.pallas as pl
import jax.experimental.pallas.tpu as pltpu

D = 8192
HD = 128
PAGE = 16
TOK = 512
FEAT = 512
CHIPS = 8
SECT = 32
SLOTS = 2
HALF = PAGE // 2
CH = TOK // 2
MSG = SLOTS * HALF
FRESH = SECT * SLOTS * PAGE
LAG = 3
ROWS = 16
NH = 4
OLD = 256
MAXP = 16
NORM_EPS = 1e-05
SCALE = HD ** -0.5
MESH = pl.DeviceIdType.MESH
F32 = jnp.float32
BF16 = jnp.bfloat16
RING = ((1, 2), (1, 1), (1, 3), (0, 2), (1, 0), (0, 1), (0, 3))
NEG = -jnp.inf
TINY = 1e-30
STEPS = 32000.0
VMEM_LIMIT = 60 * 2**20


def dot(a, b):
    return lax.dot_general(a, b, (((1,), (0,)), ((), ())), preferred_element_type=F32)


def dot_t(a, b):
    return lax.dot_general(a, b, (((1,), (1,)), ((), ())), preferred_element_type=F32)


def softmax_weights(scores):
    peak = jnp.max(scores, axis=-1, keepdims=True)
    raised = jnp.exp(scores - peak)
    return (raised * (1.0 / jnp.sum(raised, axis=-1, keepdims=True))).astype(BF16)


def kernel(
    hid, gain, weight, qpre, doc, pdest, oldp, qdec, table, ctx,
    o_pre, o_dec,
    hraw, graw, wv, docv, pdv, tabv, ctxs, hs, st, part, sibp, sbuf, rs, sstat, rstat, chooser, kvc, outg, kvh, pool,
    oldbuf, oldkv, qp, qd, pos, obuf, dbuf,
    in_sem, w_sem, sib_s, sib_r, ps_s, ps_r, rs_s, rs_r, sq_s, sq_r, aa_s, aa_r, out_sem, flood,
):
    s = lax.axis_index("sect")
    t = lax.axis_index("tp")
    k = t % 2
    x = (t // 2) % 4
    yh = t // 8
    g = t // 2
    z = s // 2
    yl = s % 2
    sib = (s, t + 1 - 2 * k)

    def ring_dst(i):
        dy, dx = RING[i]
        return ((yh + dy) % 2) * 4 + (x + dx) % 4

    def ring_src(i):
        dy, dx = RING[i]
        return ((yh + dy) % 2) * 4 + (x + 4 - dx) % 4

    def sect_peer(i):
        j = i // 2
        sign = 1 - 2 * (j % 2)
        dz = 8 + sign * ((j + 1) // 2)
        yx = 1 - i % 2
        return dz, yx

    def z_peer(dz, yx):
        return (((z + dz + 16) % 16) * 2 + (yl + yx) % 2, t)

    def remote(src, dst, ss, rr, dev):
        c = pltpu.make_async_remote_copy(
            src_ref=src, dst_ref=dst, send_sem=ss, recv_sem=rr, device_id=dev, device_id_type=MESH
        )
        c.start()
        return c

    def load(src, dst, sem):
        c = pltpu.make_async_copy(src, dst, sem)
        c.start()
        return c

    bar = pltpu.get_barrier_semaphore()
    greeted = [sib] + [(s, ring_dst(i) * 2 + k) for i in range(7)]
    greeted += [z_peer(1, 0), z_peer(-1, 0), z_peer(1, 1), z_peer(-1, 1), z_peer(0, 1)]
    for peer in greeted:
        pl.semaphore_signal(bar, inc=1, device_id=peer, device_id_type=MESH)

    order = [ring_dst(i) for i in range(7)] + [g]
    c_hid = load(hid, hraw, in_sem.at[0])
    c_gain = load(gain, graw, in_sem.at[1])
    c_w = [
        load(
            weight.at[:, pl.ds(pl.multiple_of(j * 2 * HD, 2 * HD), 2 * HD)], wv.at[j], w_sem.at[n]
        )
        for n, j in enumerate(order)
    ]
    c_pd = load(pdest, pdv, in_sem.at[2])
    c_doc = load(doc, docv, in_sem.at[3])
    c_tab = load(table, tabv, in_sem.at[4])
    c_ctx = load(ctx, ctxs, in_sem.at[5])
    c_old = load(oldp, oldbuf, in_sem.at[6])
    c_qp = load(qpre, qp, in_sem.at[7])
    c_qd = load(qdec, qd, in_sem.at[8])

    c_hid.wait()
    c_gain.wait()
    h = hraw[...].astype(F32).reshape(TOK // PAGE, PAGE, FEAT)
    h = jnp.concatenate([h[:, :HALF].reshape(CH, FEAT), h[:, HALF:].reshape(CH, FEAT)], axis=0)
    hs[...] = (h * graw[...].astype(F32).reshape(1, FEAT)).astype(BF16)
    hh = h * h
    folded = hh[:, 0:128] + hh[:, 128:256] + hh[:, 256:384] + hh[:, 384:512]
    sq_row = jnp.sum(folded.T, axis=0, keepdims=True)
    for q in range(4):
        st[k, q:q + 1, :] = sq_row[:, q * 128:(q + 1) * 128]
    st[k, 4:8, :] = jnp.zeros((4, 128), F32)

    blocks = [(c, n) for c in range(2) for n in range(8)]
    c_ps, c_rs, c_sq = {}, {}, {}
    c_st = None

    def signal_round(r):
        for sign in (1, -1):
            pl.semaphore_signal(
                flood.at[r], inc=1, device_id=z_peer(sign * (1 << r), 0), device_id_type=MESH
            )

    for q in range(16 + LAG):
        if q < 16:
            c, n = blocks[q]
            j = order[n]
            if c == 0:
                c_w[n].wait()
            both = dot(hs[c * CH:(c + 1) * CH, :], wv[j])
            part[c, j, 0] = both[:, :HD]
            part[c, j, 1] = both[:, HD:]
            if q == 0:
                pl.semaphore_wait(bar, len(greeted))
                c_st = remote(st.at[k], st.at[k], sib_s.at[0], sib_r.at[0], sib)
            c_ps[q] = remote(part.at[c, j, 1 - k], sibp.at[c, j], ps_s.at[q], ps_r.at[q], sib)
            if q == 0:
                signal_round(0)
        p = q - LAG
        if p < 0:
            continue
        if p == 0:
            c_st.wait_recv()
            chip_sq = st[0] + st[1]
            chip_col = lax.rsqrt(chip_sq * (1.0 / (2 * FEAT)) + TINY).T
        c, n = blocks[p]
        j = order[n]
        c_ps[p].wait_recv()
        total = part[c, j, k] + sibp[c, j]
        if n == 7:
            part[c, j, k] = total
            continue
        level = jnp.concatenate(
            [total[:128] * chip_col[:, 2 * c:2 * c + 1], total[128:] * chip_col[:, 2 * c + 1:2 * c + 2]],
            axis=0,
        )
        top = jnp.maximum(jnp.max(jnp.abs(level), axis=0, keepdims=True), TINY)
        sbuf[c, j] = jnp.round(level * (STEPS / top)).astype(jnp.int32).astype(jnp.int16)
        sstat[c, j] = chip_sq
        sstat[c, j, 4:5, :] = top * (1.0 / STEPS)
        peer = (s, j * 2 + k)
        c_sq[p] = remote(sstat.at[c, j], rstat.at[c, g], sq_s.at[c, n], sq_r.at[c, n], peer)
        c_rs[p] = remote(sbuf.at[c, j], rs.at[c, g], rs_s.at[c, n], rs_r.at[c, n], peer)

    pl.semaphore_wait(flood.at[0], 2)
    signal_round(1)

    c_pd.wait()
    eye = lax.broadcasted_iota(jnp.int32, (32, 32), 0) == lax.broadcasted_iota(jnp.int32, (32, 32), 1)
    page_col = jnp.sum(jnp.where(eye, jnp.broadcast_to(pdv[...], (32, 32)), 0), axis=1, keepdims=True)
    page_of = lax.broadcasted_iota(jnp.int32, (32, CH), 1) // HALF
    page_row = lax.broadcasted_iota(jnp.int32, (32, CH), 0)
    page_b = jnp.broadcast_to(page_col, (32, CH))
    dest_tok = jnp.sum(jnp.where(page_of == page_row, page_b, 0), axis=0, keepdims=True)
    rank_tok = jnp.sum(
        jnp.where((page_b == dest_tok) & (page_row < page_of), 1, 0), axis=0, keepdims=True
    )
    tok_in = lax.broadcasted_iota(jnp.int32, (1, CH), 1) % HALF
    target = (dest_tok * SLOTS + rank_tok) * HALF + tok_in
    for c in range(4):
        rows = lax.broadcasted_iota(jnp.int32, (128, CH), 0) + c * 128
        chooser[c * 128:(c + 1) * 128, :] = jnp.where(rows == target, 1.0, 0.0).astype(BF16)

    c_old.wait()
    for c in range(OLD // 32):
        blk = oldbuf[2 * c:2 * c + 2].reshape(32, 16, HD).astype(F32)
        head = lax.broadcasted_iota(jnp.int32, (1, 16, 1), 1)
        for m in range(2):
            one = jnp.sum(jnp.where(head == 2 * g + m, blk, 0.0), axis=1)
            oldkv[m, c * 32:(c + 1) * 32, :] = one.astype(BF16)

    pl.semaphore_wait(flood.at[1], 2)
    signal_round(2)

    c_tab.wait()
    c_ctx.wait()
    col = lax.broadcasted_iota(jnp.int32, (ROWS, OLD + FRESH), 1)
    fresh = col - OLD
    within = fresh % (FRESH // 2)
    col_slot = jnp.where(col < OLD, col // PAGE, 16 + within // HALF)
    col_in = jnp.where(col < OLD, col % PAGE, (fresh // (FRESH // 2)) * HALF + within % HALF)
    where_pos = jnp.full((ROWS, OLD + FRESH), 1 << 20, jnp.int32)
    tab = tabv[...]
    for j in range(MAXP):
        where_pos = jnp.where(tab[:, j:j + 1] == col_slot, j * PAGE + col_in, where_pos)
    row_id = lax.broadcasted_iota(jnp.int32, (ROWS, 1), 0)
    lens = jnp.zeros((ROWS, 1), jnp.int32)
    for r in range(ROWS):
        lens = jnp.where(row_id == r, ctxs[r], lens)
    pos[...] = jnp.where(where_pos < lens, 0.0, NEG)

    def page_copy(c, i):
        dz, yx = sect_peer(i)
        dst = ((z + dz) % 16) * 2 + (yl + yx) % 2
        return pltpu.make_async_remote_copy(
            src_ref=outg.at[c, pl.ds(pl.multiple_of(dst * MSG, MSG), MSG)],
            dst_ref=pool.at[k, c, pl.ds(pl.multiple_of(s * MSG, MSG), MSG)],
            send_sem=aa_s.at[c, i], recv_sem=aa_r.at[c, i], device_id=(dst, t), device_id_type=MESH,
        )

    def page_start(c):
        def body(i, _):
            page_copy(c, i).start()
            return 0
        lax.fori_loop(0, 31, body, 0)

    def page_wait(c):
        def body(i, _):
            page_copy(c, i).wait_recv()
            return 0
        lax.fori_loop(0, 31, body, 0)

    def page_sent(c):
        def body(i, _):
            page_copy(c, i).wait_send()
            return 0
        lax.fori_loop(0, 31, body, 0)

    own = pl.ds(pl.multiple_of(s * MSG, MSG), MSG)
    for c in range(2):
        upper = part[c, g, k, 0:128]
        lower = part[c, g, k, 128:256]
        total_sq = chip_sq
        for i in (5, 6, 3, 4, 1, 2, 0):
            p = c * 8 + i
            c_sq[p].wait_recv()
            src = ring_src(i)
            stat = rstat[c, src]
            total_sq = total_sq + stat
            ms = stat * (1.0 / (2 * FEAT)) + TINY
            scale = (ms * lax.rsqrt(ms)).T
            col_scale = stat[4:5, :]
            c_rs[p].wait_recv()
            got = rs[c, src].astype(jnp.int32).astype(F32) * col_scale
            upper = upper + got[:128] * scale[:, 2 * c:2 * c + 1]
            lower = lower + got[128:] * scale[:, 2 * c + 1:2 * c + 2]
        inv = lax.rsqrt(total_sq / D + NORM_EPS).T
        kvc[c, 0:128] = (upper * inv[:, 2 * c:2 * c + 1]).astype(BF16)
        kvc[c, 128:256] = (lower * inv[:, 2 * c + 1:2 * c + 2]).astype(BF16)
        if c == 0:
            pl.semaphore_wait(flood.at[2], 2)
        for r in range(2):
            outg[c, r * 256:(r + 1) * 256] = dot(chooser[r * 256:(r + 1) * 256, :], kvc[c]).astype(BF16)
        page_start(c)
        pool[k, c, own, :] = outg[c, own, :]
    halves = [kvc[c].astype(F32).reshape(TOK // PAGE, HALF, HD) for c in range(2)]
    kvh[k] = jnp.concatenate(halves, axis=1).reshape(TOK, HD).astype(BF16)
    c_kv = remote(kvh.at[k], kvh.at[k], sib_s.at[1], sib_r.at[1], sib)

    c_qp.wait()
    c_doc.wait()
    doc_row = docv[...].astype(F32)
    doc_col = jnp.broadcast_to(doc_row, (8, TOK)).T[:, 0:1]
    c_kv.wait_recv()
    out_copies = []
    for b in range(4):
        lo, hi = max(0, b - 2) * 128, (b + 1) * 128
        q0 = b * 128
        tq = lax.broadcasted_iota(jnp.int32, (128, hi - lo), 0) + q0
        tk = lax.broadcasted_iota(jnp.int32, (128, hi - lo), 1) + lo
        allowed = (doc_col[q0:hi, :] == doc_row[:, lo:hi]) & (tk <= tq)
        keys = kvh[0, lo:hi, :]
        values = kvh[1, lo:hi, :]
        for n in range(NH):
            sc = dot_t(qp[q0:hi, n * HD:(n + 1) * HD], keys) * SCALE
            wts = softmax_weights(jnp.where(allowed, sc, NEG))
            obuf[q0:hi, n * HD:(n + 1) * HD] = dot(wts, values).astype(BF16)
        out_copies.append(load(obuf.at[q0:hi], o_pre.at[q0:hi], out_sem.at[b]))

    c_qd.wait()
    qs = jnp.concatenate([qd[:, n * HD:(n + 1) * HD] for n in range(NH)], axis=0)
    mask = jnp.concatenate([pos[...]] * NH, axis=0)
    score = [dot_t(qs, oldkv[0]) * SCALE + mask[:, :OLD]]
    peak = jnp.max(score[0], axis=-1, keepdims=True)
    half = FRESH // 2
    c_pool = []
    for c in range(2):
        page_wait(c)
        c_pool.append(remote(pool.at[k, c], pool.at[k, c], sib_s.at[2 + c], sib_r.at[2 + c], sib))
    for c in range(2):
        c_pool[c].wait_recv()
        sc = dot_t(qs, pool[0, c]) * SCALE + mask[:, OLD + c * half:OLD + (c + 1) * half]
        score.append(sc)
        peak = jnp.maximum(peak, jnp.max(sc, axis=-1, keepdims=True))
    raised = [jnp.exp(sc - peak) for sc in score]
    norm = sum(jnp.sum(e, axis=-1, keepdims=True) for e in raised)
    norm = 1.0 / norm
    mixed = dot((raised[0] * norm).astype(BF16), oldkv[1])
    for c in range(2):
        mixed = mixed + dot((raised[1 + c] * norm).astype(BF16), pool[1, c])
    mixed = mixed.astype(BF16)
    for n in range(NH):
        dbuf[:, n * HD:(n + 1) * HD] = mixed[n * ROWS:(n + 1) * ROWS]
    out_copies.append(load(dbuf, o_dec, out_sem.at[4]))

    for c in [c_st, c_kv] + c_pool + list(c_ps.values()) + list(c_rs.values()) + list(c_sq.values()):
        c.wait_send()
    page_sent(0)
    page_sent(1)
    for c in out_copies:
        c.wait()


def local(hidden_pre, norm_gain, kv_weight, query_pre, doc_ids, page_dest, old_pages, query_dec, page_table, ctx_len):
    any_spec = pl.BlockSpec(memory_space=pl.ANY)
    dma = pltpu.SemaphoreType.DMA
    vm = pltpu.VMEM
    I32 = jnp.int32
    I16 = jnp.int16
    return pl.pallas_call(
        kernel,
        name="serve",
        out_shape=(
            jax.ShapeDtypeStruct((TOK, NH * HD), BF16),
            jax.ShapeDtypeStruct((ROWS, NH * HD), BF16),
        ),
        in_specs=[any_spec] * 10,
        out_specs=(any_spec, any_spec),
        scratch_shapes=[
            vm((TOK, FEAT), BF16), vm((FEAT,), BF16), vm((CHIPS, FEAT, 2 * HD), BF16),
            vm((1, TOK), I32), vm((1, 32), I32), vm((ROWS, MAXP), I32), pltpu.SMEM((ROWS,), I32),
            vm((TOK, FEAT), BF16), vm((2, 8, 128), F32),
            vm((2, CHIPS, 2, CH, HD), F32), vm((2, CHIPS, CH, HD), F32),
            vm((2, CHIPS, CH, HD), I16), vm((2, CHIPS, CH, HD), I16),
            vm((2, CHIPS, 8, HD), F32), vm((2, CHIPS, 8, HD), F32),
            vm((FRESH // 2, CH), BF16), vm((2, CH, HD), BF16), vm((2, FRESH // 2, HD), BF16),
            vm((2, TOK, HD), BF16), vm((2, 2, FRESH // 2, HD), BF16),
            vm((16, 16, 16, HD), BF16), vm((2, OLD, HD), BF16), vm((TOK, NH * HD), BF16),
            vm((ROWS, NH * HD), BF16), vm((ROWS, OLD + FRESH), F32),
            vm((TOK, NH * HD), BF16), vm((ROWS, NH * HD), BF16),
            dma((9,)), dma((8,)), dma((4,)), dma((4,)), dma((16,)), dma((16,)), dma((2, 7)), dma((2, 7)),
            dma((2, 7)), dma((2, 7)), dma((2, 31)), dma((2, 31)), dma((5,)), pltpu.SemaphoreType.REGULAR((3,)),
        ],
        compiler_params=pltpu.CompilerParams(
            collective_id=0, has_side_effects=True, vmem_limit_bytes=VMEM_LIMIT
        ),
    )(
        hidden_pre, norm_gain, kv_weight, query_pre, doc_ids, page_dest.reshape(1, 32), old_pages,
        query_dec, page_table, ctx_len,
    )


def solution(mesh):
    in_specs = (
        P("sect", "tp"),
        P("tp"),
        P("tp", None),
        P("sect", "tp"),
        P("sect", None),
        P("sect", None),
        P("sect", None, None, None),
        P("sect", "tp"),
        P("sect", None),
        P("sect"),
    )
    out_specs = (P("sect", "tp"), P("sect", "tp"))
    return jax.shard_map(local, mesh=mesh, in_specs=in_specs, out_specs=out_specs, check_vma=False)
```

```python
import jax
import jax.numpy as jnp
from jax import lax
from jax.sharding import PartitionSpec as P
import jax.experimental.pallas as pl
import jax.experimental.pallas.tpu as pltpu

D = 8192
HD = 128
PAGE = 16
TOK = 512
FEAT = 512
CHIPS = 8
SECT = 32
SLOTS = 2
HALF = PAGE // 2
CH = TOK // 2
MSG = SLOTS * HALF
FRESH = SECT * SLOTS * PAGE
LAG = 3
AHEAD = 6
ROWS = 16
NH = 4
OLD = 256
MAXP = 16
NORM_EPS = 1e-05
SCALE = HD ** -0.5
MESH = pl.DeviceIdType.MESH
F32 = jnp.float32
BF16 = jnp.bfloat16
RING = ((1, 2), (1, 1), (1, 3), (0, 2), (1, 0), (0, 1), (0, 3))
NEG = -jnp.inf
TINY = 1e-30
STEPS = 32000.0
VMEM_LIMIT = 60 * 2**20


def dot(a, b):
    return lax.dot_general(a, b, (((1,), (0,)), ((), ())), preferred_element_type=F32)


def dot_t(a, b):
    return lax.dot_general(a, b, (((1,), (1,)), ((), ())), preferred_element_type=F32)


def softmax_weights(scores):
    peak = jnp.max(scores, axis=-1, keepdims=True)
    raised = jnp.exp(scores - peak)
    return (raised * (1.0 / jnp.sum(raised, axis=-1, keepdims=True))).astype(BF16)


def kernel(
    hid, gain, weight, qpre, doc, pdest, oldp, qdec, table, ctx,
    o_pre, o_dec,
    hraw, graw, wv, docv, pdv, tabv, ctxs, hs, st, part, sibp, sbuf, rs, sstat, rstat, chooser, kvc, outg, kvh, pool,
    oldbuf, oldkv, qp, qd, pos, obuf, dbuf,
    in_sem, w_sem, sib_s, sib_r, ps_s, ps_r, rs_s, rs_r, sq_s, sq_r, aa_s, aa_r, out_sem, flood,
):
    s = lax.axis_index("sect")
    t = lax.axis_index("tp")
    k = t % 2
    x = (t // 2) % 4
    yh = t // 8
    g = t // 2
    z = s // 2
    yl = s % 2
    sib = (s, t + 1 - 2 * k)

    def ring_dst(i):
        dy, dx = RING[i]
        return ((yh + dy) % 2) * 4 + (x + dx) % 4

    def ring_src(i):
        dy, dx = RING[i]
        return ((yh + dy) % 2) * 4 + (x + 4 - dx) % 4

    def z_peer(dz, yx):
        return (((z + dz + 16) % 16) * 2 + (yl + yx) % 2, t)

    def remote(src, dst, ss, rr, dev):
        c = pltpu.make_async_remote_copy(
            src_ref=src, dst_ref=dst, send_sem=ss, recv_sem=rr, device_id=dev, device_id_type=MESH
        )
        c.start()
        return c

    def load(src, dst, sem):
        c = pltpu.make_async_copy(src, dst, sem)
        c.start()
        return c

    bar = pltpu.get_barrier_semaphore()
    greeted = [sib] + [(s, ring_dst(i) * 2 + k) for i in range(7)]
    greeted += [z_peer(1, 0), z_peer(-1, 0), z_peer(1, 1), z_peer(-1, 1), z_peer(0, 1)]
    for peer in greeted:
        pl.semaphore_signal(bar, inc=1, device_id=peer, device_id_type=MESH)

    order = [ring_dst(i) for i in range(7)] + [g]
    c_hid = load(hid, hraw, in_sem.at[0])
    c_gain = load(gain, graw, in_sem.at[1])
    c_w = [
        load(
            weight.at[:, pl.ds(pl.multiple_of(j * 2 * HD, 2 * HD), 2 * HD)], wv.at[j], w_sem.at[n]
        )
        for n, j in enumerate(order)
    ]
    c_pd = load(pdest, pdv, in_sem.at[2])
    c_doc = load(doc, docv, in_sem.at[3])
    c_tab = load(table, tabv, in_sem.at[4])
    c_ctx = load(ctx, ctxs, in_sem.at[5])
    c_old = load(oldp, oldbuf, in_sem.at[6])
    c_qp = load(qpre, qp, in_sem.at[7])
    c_qd = load(qdec, qd, in_sem.at[8])

    c_hid.wait()
    c_gain.wait()
    h = hraw[...].astype(F32).reshape(TOK // PAGE, PAGE, FEAT)
    h = jnp.concatenate([h[:, :HALF].reshape(CH, FEAT), h[:, HALF:].reshape(CH, FEAT)], axis=0)
    hs[...] = (h * graw[...].astype(F32).reshape(1, FEAT)).astype(BF16)
    hh = h * h
    folded = hh[:, 0:128] + hh[:, 128:256] + hh[:, 256:384] + hh[:, 384:512]
    sq_row = jnp.sum(folded.T, axis=0, keepdims=True)
    for q in range(4):
        st[k, q:q + 1, :] = sq_row[:, q * 128:(q + 1) * 128]
    st[k, 4:8, :] = jnp.zeros((4, 128), F32)

    blocks = [(c, n) for c in range(2) for n in range(8)]
    c_ps, c_rs, c_sq = {}, {}, {}
    c_st = None

    def signal_round(r):
        for sign in (1, -1):
            pl.semaphore_signal(
                flood.at[r], inc=1, device_id=z_peer(sign * (1 << r), 0), device_id_type=MESH
            )

    def swap(q):
        c, n = blocks[q]
        j = order[n]
        c_ps[q] = remote(part.at[c, j, 1 - k], sibp.at[c, j], ps_s.at[q], ps_r.at[q], sib)

    done = 0
    for q in range(16 + LAG):
        if q < 16:
            c, n = blocks[q]
            j = order[n]
            if c == 0:
                c_w[n].wait()
            both = dot(hs[c * CH:(c + 1) * CH, :], wv[j])
            part[c, j, 0] = both[:, :HD]
            part[c, j, 1] = both[:, HD:]
        if q < AHEAD - 1:
            continue
        if q == AHEAD - 1:
            pl.semaphore_wait(bar, len(greeted))
            c_st = remote(st.at[k], st.at[k], sib_s.at[0], sib_r.at[0], sib)
            signal_round(0)
            for early in range(AHEAD):
                swap(early)
        elif q < 16:
            swap(q)
        while done <= q - LAG:
            p = done
            done += 1
            if p == 0:
                c_st.wait_recv()
                chip_sq = st[0] + st[1]
                chip_col = lax.rsqrt(chip_sq * (1.0 / (2 * FEAT)) + TINY).T
            c, n = blocks[p]
            j = order[n]
            c_ps[p].wait_recv()
            total = part[c, j, k] + sibp[c, j]
            if n == 7:
                part[c, j, k] = total
                continue
            level = jnp.concatenate(
                [
                    total[:128] * chip_col[:, 2 * c:2 * c + 1],
                    total[128:] * chip_col[:, 2 * c + 1:2 * c + 2],
                ],
                axis=0,
            )
            top = jnp.maximum(jnp.max(jnp.abs(level), axis=0, keepdims=True), TINY)
            sbuf[c, j] = jnp.round(level * (STEPS / top)).astype(jnp.int32).astype(jnp.int16)
            sstat[c, j] = chip_sq
            sstat[c, j, 4:5, :] = top * (1.0 / STEPS)
            peer = (s, j * 2 + k)
            c_sq[p] = remote(sstat.at[c, j], rstat.at[c, g], sq_s.at[c, n], sq_r.at[c, n], peer)
            c_rs[p] = remote(sbuf.at[c, j], rs.at[c, g], rs_s.at[c, n], rs_r.at[c, n], peer)
        if q == 10:
            pl.semaphore_wait(flood.at[0], 2)
            signal_round(1)

    c_pd.wait()
    eye = lax.broadcasted_iota(jnp.int32, (32, 32), 0) == lax.broadcasted_iota(jnp.int32, (32, 32), 1)
    page_col = jnp.sum(jnp.where(eye, jnp.broadcast_to(pdv[...], (32, 32)), 0), axis=1, keepdims=True)
    page_of = lax.broadcasted_iota(jnp.int32, (32, CH), 1) // HALF
    page_row = lax.broadcasted_iota(jnp.int32, (32, CH), 0)
    page_b = jnp.broadcast_to(page_col, (32, CH))
    dest_tok = jnp.sum(jnp.where(page_of == page_row, page_b, 0), axis=0, keepdims=True)
    rank_tok = jnp.sum(
        jnp.where((page_b == dest_tok) & (page_row < page_of), 1, 0), axis=0, keepdims=True
    )
    tok_in = lax.broadcasted_iota(jnp.int32, (1, CH), 1) % HALF
    target = (dest_tok * SLOTS + rank_tok) * HALF + tok_in
    for c in range(4):
        rows = lax.broadcasted_iota(jnp.int32, (128, CH), 0) + c * 128
        chooser[c * 128:(c + 1) * 128, :] = jnp.where(rows == target, 1.0, 0.0).astype(BF16)

    c_old.wait()
    for c in range(OLD // 32):
        blk = oldbuf[2 * c:2 * c + 2].reshape(32, 16, HD).astype(F32)
        head = lax.broadcasted_iota(jnp.int32, (1, 16, 1), 1)
        for m in range(2):
            one = jnp.sum(jnp.where(head == 2 * g + m, blk, 0.0), axis=1)
            oldkv[m, c * 32:(c + 1) * 32, :] = one.astype(BF16)

    pl.semaphore_wait(flood.at[1], 2)
    signal_round(2)

    c_tab.wait()
    c_ctx.wait()
    col = lax.broadcasted_iota(jnp.int32, (ROWS, OLD + FRESH), 1)
    fresh = col - OLD
    within = fresh % (FRESH // 2)
    col_slot = jnp.where(col < OLD, col // PAGE, 16 + within // HALF)
    col_in = jnp.where(col < OLD, col % PAGE, (fresh // (FRESH // 2)) * HALF + within % HALF)
    where_pos = jnp.full((ROWS, OLD + FRESH), 1 << 20, jnp.int32)
    tab = tabv[...]
    for j in range(MAXP):
        where_pos = jnp.where(tab[:, j:j + 1] == col_slot, j * PAGE + col_in, where_pos)
    row_id = lax.broadcasted_iota(jnp.int32, (ROWS, 1), 0)
    lens = jnp.zeros((ROWS, 1), jnp.int32)
    for r in range(ROWS):
        lens = jnp.where(row_id == r, ctxs[r], lens)
    pos[...] = jnp.where(where_pos < lens, 0.0, NEG)

    def page_copy(c, i):
        dst = i + (SECT + i - s) // SECT
        return pltpu.make_async_remote_copy(
            src_ref=outg.at[c, pl.ds(pl.multiple_of(dst * MSG, MSG), MSG)],
            dst_ref=pool.at[k, c, pl.ds(pl.multiple_of(s * MSG, MSG), MSG)],
            send_sem=aa_s.at[c], recv_sem=aa_r.at[c], device_id=(dst, t), device_id_type=MESH,
        )

    def page_start(c):
        def body(i, _):
            page_copy(c, i).start()
            return 0
        lax.fori_loop(0, 31, body, 0)

    def pages_all(c):
        most = pl.ds(0, 31 * MSG)
        return pltpu.make_async_remote_copy(
            src_ref=outg.at[c, most], dst_ref=pool.at[k, c, most],
            send_sem=aa_s.at[c], recv_sem=aa_r.at[c], device_id=sib, device_id_type=MESH,
        )

    own = pl.ds(pl.multiple_of(s * MSG, MSG), MSG)
    total_sq = chip_sq
    scales = {}
    for c in range(2):
        upper = part[c, g, k, 0:128]
        lower = part[c, g, k, 128:256]
        for i in (5, 6, 3, 4, 1, 2, 0):
            p = c * 8 + i
            c_sq[p].wait_recv()
            src = ring_src(i)
            stat = rstat[c, src]
            if c == 0:
                total_sq = total_sq + stat
                ms = stat * (1.0 / (2 * FEAT)) + TINY
                scales[i] = (ms * lax.rsqrt(ms)).T
            col_scale = stat[4:5, :]
            c_rs[p].wait_recv()
            got = rs[c, src].astype(jnp.int32).astype(F32) * col_scale
            upper = upper + got[:128] * scales[i][:, 2 * c:2 * c + 1]
            lower = lower + got[128:] * scales[i][:, 2 * c + 1:2 * c + 2]
        if c == 0:
            inv = lax.rsqrt(total_sq / D + NORM_EPS).T
        kvc[c, 0:128] = (upper * inv[:, 2 * c:2 * c + 1]).astype(BF16)
        kvc[c, 128:256] = (lower * inv[:, 2 * c + 1:2 * c + 2]).astype(BF16)
        if c == 0:
            pl.semaphore_wait(flood.at[2], 2)
        for r in range(2):
            outg[c, r * 256:(r + 1) * 256] = dot(chooser[r * 256:(r + 1) * 256, :], kvc[c]).astype(BF16)
        page_start(c)
        pool[k, c, own, :] = outg[c, own, :]
    halves = [kvc[c].astype(F32).reshape(TOK // PAGE, HALF, HD) for c in range(2)]
    kvh[k] = jnp.concatenate(halves, axis=1).reshape(TOK, HD).astype(BF16)
    c_kv = remote(kvh.at[k], kvh.at[k], sib_s.at[1], sib_r.at[1], sib)

    c_qp.wait()
    c_doc.wait()
    doc_row = docv[...].astype(F32)
    doc_col = jnp.broadcast_to(doc_row, (8, TOK)).T[:, 0:1]
    c_kv.wait_recv()
    out_copies = []
    for b in range(4):
        lo, hi = max(0, b - 2) * 128, (b + 1) * 128
        q0 = b * 128
        tq = lax.broadcasted_iota(jnp.int32, (128, hi - lo), 0) + q0
        tk = lax.broadcasted_iota(jnp.int32, (128, hi - lo), 1) + lo
        allowed = (doc_col[q0:hi, :] == doc_row[:, lo:hi]) & (tk <= tq)
        keys = kvh[0, lo:hi, :]
        values = kvh[1, lo:hi, :]
        for n in range(NH):
            sc = dot_t(qp[q0:hi, n * HD:(n + 1) * HD], keys) * SCALE
            wts = softmax_weights(jnp.where(allowed, sc, NEG))
            obuf[q0:hi, n * HD:(n + 1) * HD] = dot(wts, values).astype(BF16)
        out_copies.append(load(obuf.at[q0:hi], o_pre.at[q0:hi], out_sem.at[b]))

    c_qd.wait()
    qs = jnp.concatenate([qd[:, n * HD:(n + 1) * HD] for n in range(NH)], axis=0)
    mask = jnp.concatenate([pos[...]] * NH, axis=0)
    score = [dot_t(qs, oldkv[0]) * SCALE + mask[:, :OLD]]
    peak = jnp.max(score[0], axis=-1, keepdims=True)
    half = FRESH // 2
    c_pool = []
    for c in [c_st] + list(c_ps.values()) + list(c_rs.values()) + list(c_sq.values()):
        c.wait_send()
    for c in range(2):
        pages_all(c).wait_recv()
        c_pool.append(remote(pool.at[k, c], pool.at[k, c], sib_s.at[2 + c], sib_r.at[2 + c], sib))
    for c in range(2):
        c_pool[c].wait_recv()
        sc = dot_t(qs, pool[0, c]) * SCALE + mask[:, OLD + c * half:OLD + (c + 1) * half]
        score.append(sc)
        peak = jnp.maximum(peak, jnp.max(sc, axis=-1, keepdims=True))
    raised = [jnp.exp(sc - peak) for sc in score]
    norm = sum(jnp.sum(e, axis=-1, keepdims=True) for e in raised)
    norm = 1.0 / norm
    mixed = dot((raised[0] * norm).astype(BF16), oldkv[1])
    for c in range(2):
        mixed = mixed + dot((raised[1 + c] * norm).astype(BF16), pool[1, c])
    mixed = mixed.astype(BF16)
    for n in range(NH):
        dbuf[:, n * HD:(n + 1) * HD] = mixed[n * ROWS:(n + 1) * ROWS]
    out_copies.append(load(dbuf, o_dec, out_sem.at[4]))

    for c in [c_kv] + c_pool:
        c.wait_send()
    for c in range(2):
        pages_all(c).wait_send()
    for c in out_copies:
        c.wait()


def local(hidden_pre, norm_gain, kv_weight, query_pre, doc_ids, page_dest, old_pages, query_dec, page_table, ctx_len):
    any_spec = pl.BlockSpec(memory_space=pl.ANY)
    dma = pltpu.SemaphoreType.DMA
    vm = pltpu.VMEM
    I32 = jnp.int32
    I16 = jnp.int16
    return pl.pallas_call(
        kernel,
        name="serve",
        out_shape=(
            jax.ShapeDtypeStruct((TOK, NH * HD), BF16),
            jax.ShapeDtypeStruct((ROWS, NH * HD), BF16),
        ),
        in_specs=[any_spec] * 10,
        out_specs=(any_spec, any_spec),
        scratch_shapes=[
            vm((TOK, FEAT), BF16), vm((FEAT,), BF16), vm((CHIPS, FEAT, 2 * HD), BF16),
            vm((1, TOK), I32), vm((1, 32), I32), vm((ROWS, MAXP), I32), pltpu.SMEM((ROWS,), I32),
            vm((TOK, FEAT), BF16), vm((2, 8, 128), F32),
            vm((2, CHIPS, 2, CH, HD), F32), vm((2, CHIPS, CH, HD), F32),
            vm((2, CHIPS, CH, HD), I16), vm((2, CHIPS, CH, HD), I16),
            vm((2, CHIPS, 8, HD), F32), vm((2, CHIPS, 8, HD), F32),
            vm((FRESH // 2, CH), BF16), vm((2, CH, HD), BF16), vm((2, FRESH // 2, HD), BF16),
            vm((2, TOK, HD), BF16), vm((2, 2, FRESH // 2, HD), BF16),
            vm((16, 16, 16, HD), BF16), vm((2, OLD, HD), BF16), vm((TOK, NH * HD), BF16),
            vm((ROWS, NH * HD), BF16), vm((ROWS, OLD + FRESH), F32),
            vm((TOK, NH * HD), BF16), vm((ROWS, NH * HD), BF16),
            dma((9,)), dma((8,)), dma((4,)), dma((4,)), dma((16,)), dma((16,)), dma((2, 7)), dma((2, 7)),
            dma((2, 7)), dma((2, 7)), dma((2,)), dma((2,)), dma((5,)), pltpu.SemaphoreType.REGULAR((3,)),
        ],
        compiler_params=pltpu.CompilerParams(
            collective_id=0, has_side_effects=True, vmem_limit_bytes=VMEM_LIMIT
        ),
    )(
        hidden_pre, norm_gain, kv_weight, query_pre, doc_ids, page_dest.reshape(1, 32), old_pages,
        query_dec, page_table, ctx_len,
    )


def solution(mesh):
    in_specs = (
        P("sect", "tp"),
        P("tp"),
        P("tp", None),
        P("sect", "tp"),
        P("sect", None),
        P("sect", None),
        P("sect", None, None, None),
        P("sect", "tp"),
        P("sect", None),
        P("sect"),
    )
    out_specs = (P("sect", "tp"), P("sect", "tp"))
    return jax.shard_map(local, mesh=mesh, in_specs=in_specs, out_specs=out_specs, check_vma=False)
```

```python
import jax
import jax.numpy as jnp
from jax import lax
from jax.sharding import PartitionSpec as P
import jax.experimental.pallas as pl
import jax.experimental.pallas.tpu as pltpu

D = 8192
HD = 128
PAGE = 16
TOK = 512
FEAT = 512
CHIPS = 8
SECT = 32
SLOTS = 2
HALF = PAGE // 2
CH = TOK // 2
MSG = SLOTS * HALF
FRESH = SECT * SLOTS * PAGE
LAG = 2
AHEAD = 3
EARLY = 6
RH = CH // 2
KEYS = ((1, 2), (0, 2), (1, 1), (0, 1), (1, 0), (1, 3), (0, 3), (0, 0))
ROWS = 16
NH = 4
OLD = 256
MAXP = 16
NORM_EPS = 1e-05
SCALE = HD ** -0.5
MESH = pl.DeviceIdType.MESH
F32 = jnp.float32
BF16 = jnp.bfloat16
NEG = -jnp.inf
TINY = 1e-30
STEPS = 32000.0
VMEM_LIMIT = 60 * 2**20


def dot(a, b):
    return lax.dot_general(a, b, (((1,), (0,)), ((), ())), preferred_element_type=F32)


def dot_t(a, b):
    return lax.dot_general(a, b, (((1,), (1,)), ((), ())), preferred_element_type=F32)


def softmax_weights(scores):
    peak = jnp.max(scores, axis=-1, keepdims=True)
    raised = jnp.exp(scores - peak)
    return (raised * (1.0 / jnp.sum(raised, axis=-1, keepdims=True))).astype(BF16)


def kernel(
    hid, gain, weight, qpre, doc, pdest, oldp, qdec, table, ctx,
    o_pre, o_dec,
    hraw, graw, wv, docv, pdv, tabv, ctxs, hs, st, part, sibp, sbuf, sbuf2, rs, nsend, nrecv, rowb, chooser, kvc, outg, kvh, pool,
    oldbuf, oldkv, qp, qd, pos, obuf,
    in_sem, w_sem, sib_s, sib_r, ps_s, ps_r, rs_s, rs_r, sq_s, sq_r, aa_s, aa_r, out_sem, flood,
):
    s = lax.axis_index("sect")
    t = lax.axis_index("tp")
    k = t % 2
    x = (t // 2) % 4
    yh = t // 8
    g = t // 2
    z = s // 2
    yl = s % 2
    sib = (s, t + 1 - 2 * k)

    def head(rel, dx):
        return ((yh + rel) % 2) * 4 + (x + dx) % 4

    def chip(rel, dx):
        return (s, head(rel, dx) * 2 + k)

    def z_peer(dz, yx):
        return (((z + dz + 16) % 16) * 2 + (yl + yx) % 2, t)

    def remote(src, dst, ss, rr, dev):
        c = pltpu.make_async_remote_copy(
            src_ref=src, dst_ref=dst, send_sem=ss, recv_sem=rr, device_id=dev, device_id_type=MESH
        )
        c.start()
        return c

    def load(src, dst, sem):
        c = pltpu.make_async_copy(src, dst, sem)
        c.start()
        return c

    bar = pltpu.get_barrier_semaphore()
    greeted = [sib, chip(1, 0), chip(0, 1), chip(0, 2), chip(0, 3)]
    greeted += [z_peer(1, 0), z_peer(-1, 0), z_peer(1, 1), z_peer(-1, 1), z_peer(0, 1)]
    for peer in greeted:
        pl.semaphore_signal(bar, inc=1, device_id=peer, device_id_type=MESH)

    c_hid = load(hid, hraw, in_sem.at[0])
    c_gain = load(gain, graw, in_sem.at[1])
    c_w = {}
    for n, key in enumerate(KEYS):
        j = head(*key)
        c_w[key] = load(
            weight.at[:, pl.ds(pl.multiple_of(j * 2 * HD, 2 * HD), 2 * HD)], wv.at[j], w_sem.at[n]
        )
    c_pd = load(pdest, pdv, in_sem.at[2])
    c_doc = load(doc, docv, in_sem.at[3])
    c_tab = load(table, tabv, in_sem.at[4])
    c_ctx = load(ctx, ctxs, in_sem.at[5])
    c_old = load(oldp, oldbuf, in_sem.at[6])
    c_qp = load(qpre, qp, in_sem.at[7])
    c_qd = load(qdec, qd, in_sem.at[8])

    c_hid.wait()
    c_gain.wait()
    h = hraw[...].astype(F32).reshape(TOK // PAGE, PAGE, FEAT)
    h = jnp.concatenate([h[:, :HALF].reshape(CH, FEAT), h[:, HALF:].reshape(CH, FEAT)], axis=0)
    hs[...] = (h * graw[...].astype(F32).reshape(1, FEAT)).astype(BF16)
    hh = h * h
    folded = hh[:, 0:128] + hh[:, 128:256] + hh[:, 256:384] + hh[:, 384:512]
    sq_row = jnp.sum(folded.T, axis=0, keepdims=True)
    for q in range(4):
        st[k, q:q + 1, :] = sq_row[:, q * 128:(q + 1) * 128]
    st[k, 4:8, :] = jnp.zeros((4, 128), F32)

    c_ps, sends, inbox, notes = {}, [], {}, {}
    nsend[...] = jnp.zeros(nsend.shape, F32)

    def signal_round(r):
        for sign in (1, -1):
            pl.semaphore_signal(
                flood.at[r], inc=1, device_id=z_peer(sign * (1 << r), 0), device_id_type=MESH
            )

    def norm_col(sq):
        return lax.rsqrt(sq * (1.0 / (2 * FEAT)) + TINY).T

    def scale_col(sq):
        ms = sq * (1.0 / (2 * FEAT)) + TINY
        return (ms * lax.rsqrt(ms)).T

    def spread(cols, quarter):
        return jnp.broadcast_to(cols[:, quarter:quarter + 1], (RH, HD))

    def code(level):
        top = jnp.maximum(jnp.max(jnp.abs(level), axis=0, keepdims=True), TINY)
        return jnp.round(level * (STEPS / top)).astype(jnp.int32).astype(jnp.int16), top * (1.0 / STEPS)

    def post(key, src, dst, index, peer):
        inbox[key] = remote(src, dst, rs_s.at[index], rs_r.at[index], peer)
        sends.append(inbox[key])

    def post_first(c, rel, dx):
        j = head(rel, dx)
        if rel == 1:
            post((c, "up", dx), sbuf.at[j, pl.ds(c * CH, RH)], rs.at[c, dx], c * 14 + dx, chip(1, 0))
        if dx > 0:
            slot = 4 + 2 * (dx - 1) + rel
            post(
                (c, "low", rel, dx), sbuf.at[j, pl.ds(c * CH + RH, RH)], rs.at[c, slot], c * 14 + slot,
                chip(0, dx),
            )

    def post_note(note, sq, lines, peer):
        nsend[note, 0:4, :] = sq[0:4]
        for line, value in lines:
            nsend[note, line:line + 1, :] = value
        notes[note] = remote(nsend.at[note], nrecv.at[note], sq_s.at[note], sq_r.at[note], peer)
        sends.append(notes[note])

    def decode(c, slot, stat, line):
        return rs[c, slot].astype(jnp.int32).astype(F32) * stat[line:line + 1, :]

    steps = {}
    done = 0
    for q in range(8 + LAG):
        if q < 8:
            j = head(*KEYS[q])
            c_w[KEYS[q]].wait()
            both = dot(hs[...], wv[j])
            part[j, 0] = both[:, :HD]
            part[j, 1] = both[:, HD:]
        if q < AHEAD - 1:
            continue
        if q == AHEAD - 1:
            pl.semaphore_wait(bar, len(greeted))
            c_st = remote(st.at[k], st.at[k], sib_s.at[0], sib_r.at[0], sib)
            signal_round(0)
        for p in range(q if q >= AHEAD else 0, q + 1):
            if p < 8:
                j = head(*KEYS[p])
                c_ps[p] = remote(part.at[j, 1 - k], sibp.at[j], ps_s.at[p], ps_r.at[p], sib)
        while done <= q - LAG:
            p = done
            done += 1
            if p == 0:
                c_st.wait_recv()
                chip_sq = st[0] + st[1]
                chip_col = norm_col(chip_sq)
                for quarter in range(4):
                    rowb[quarter * RH:(quarter + 1) * RH] = spread(chip_col, quarter)
            rel, dx = KEYS[p]
            j = head(rel, dx)
            c_ps[p].wait_recv()
            total = part[j, k] + sibp[j]
            part[j, k] = total
            if (rel, dx) == (0, 0):
                continue
            if p == 2:
                pl.semaphore_wait(flood.at[0], 2)
                signal_round(1)
            sbuf[j], steps[rel, dx] = code(total * rowb[...])
            post_first(0, rel, dx)
            if (rel, dx) == (1, 3):
                post_note(0, chip_sq, [(4 + n, steps[1, n]) for n in range(4)], chip(1, 0))
            if rel == 0:
                post_note(dx, chip_sq, [(4, steps[0, dx]), (5, steps[1, dx])], chip(0, dx))
    for rel, dx in KEYS:
        post_first(1, rel, dx)
    pl.semaphore_wait(flood.at[1], 2)
    signal_round(2)

    known = {}

    def second_step(c):
        if c == 0:
            notes[0].wait_recv()
            stat = nrecv[0]
            known["row_sq"] = chip_sq + stat
            known["row_col"] = norm_col(known["row_sq"])
            known["up"] = scale_col(stat)
        for dx in (2, 1, 3):
            inbox[c, "up", dx].wait_recv()
        scale = spread(known["up"], 2 * c)
        norm = spread(known["row_col"], 2 * c)
        lines = {}
        for dx in (2, 1, 3):
            value = decode(c, dx, nrecv[0], 4 + dx) * scale + part[head(0, dx), k, c * CH:c * CH + RH]
            sbuf2[c, dx - 1], lines[dx] = code(value * norm)
        for dx in (2, 1, 3):
            post((c, dx), sbuf2.at[c, dx - 1], rs.at[c, 9 + dx], c * 14 + 9 + dx, chip(0, dx))
            post_note(3 + 4 * c + dx, known["row_sq"], [(4, lines[dx])], chip(0, dx))
        if c == 0:
            quad_sq = chip_sq
            for dx in (2, 1, 3):
                notes[dx].wait_recv()
                stat = nrecv[dx]
                known[dx] = scale_col(stat)
                quad_sq = quad_sq + stat
            known["quad_sq"] = quad_sq
            known["quad_col"] = norm_col(quad_sq)
        for dx in (2, 1, 3):
            inbox[c, "low", 1, dx].wait_recv()
        value = part[head(1, 0), k, c * CH + RH:(c + 1) * CH]
        for dx in (2, 1, 3):
            value = value + decode(c, 5 + 2 * (dx - 1), nrecv[dx], 5) * spread(known[dx], 2 * c + 1)
        sbuf2[c, 3], line = code(value * spread(known["quad_col"], 2 * c + 1))
        post((c, 13), sbuf2.at[c, 3], rs.at[c, 13], c * 14 + 13, chip(1, 0))
        post_note(7 + 4 * c, known["quad_sq"], [(4, line)], chip(1, 0))

    def last_step(c):
        for dx in (1, 3, 2):
            notes[3 + 4 * c + dx].wait_recv()
        if c == 0:
            total_sq = known["row_sq"]
            for dx in (1, 3, 2):
                known[3 + dx] = scale_col(nrecv[3 + dx])
                total_sq = total_sq + nrecv[3 + dx]
            known["inv"] = lax.rsqrt(total_sq / D + NORM_EPS).T
        inbox[c, "up", 0].wait_recv()
        for dx in (1, 2, 3):
            inbox[c, "low", 0, dx].wait_recv()
            inbox[c, dx].wait_recv()
        notes[7 + 4 * c].wait_recv()
        inbox[c, 13].wait_recv()
        if c == 0:
            known[7] = scale_col(nrecv[7])
        top = decode(c, 0, nrecv[0], 4) * spread(known["up"], 2 * c) + part[g, k, c * CH:c * CH + RH]
        low = part[g, k, c * CH + RH:(c + 1) * CH]
        for dx in (1, 3, 2):
            top = top + decode(c, 9 + dx, nrecv[3 + 4 * c + dx], 4) * spread(known[3 + dx], 2 * c)
            low = low + decode(c, 4 + 2 * (dx - 1), nrecv[dx], 4) * spread(known[dx], 2 * c + 1)
        low = low + decode(c, 13, nrecv[7 + 4 * c], 4) * spread(known[7], 2 * c + 1)
        kvc[c, 0:RH] = (top * spread(known["inv"], 2 * c)).astype(BF16)
        kvc[c, RH:CH] = (low * spread(known["inv"], 2 * c + 1)).astype(BF16)

    c_pd.wait()
    eye = lax.broadcasted_iota(jnp.int32, (32, 32), 0) == lax.broadcasted_iota(jnp.int32, (32, 32), 1)
    page_col = jnp.sum(jnp.where(eye, jnp.broadcast_to(pdv[...], (32, 32)), 0), axis=1, keepdims=True)
    page_of = lax.broadcasted_iota(jnp.int32, (32, CH), 1) // HALF
    page_row = lax.broadcasted_iota(jnp.int32, (32, CH), 0)
    page_b = jnp.broadcast_to(page_col, (32, CH))
    dest_tok = jnp.sum(jnp.where(page_of == page_row, page_b, 0), axis=0, keepdims=True)
    rank_tok = jnp.sum(
        jnp.where((page_b == dest_tok) & (page_row < page_of), 1, 0), axis=0, keepdims=True
    )
    tok_in = lax.broadcasted_iota(jnp.int32, (1, CH), 1) % HALF
    target = (dest_tok * SLOTS + rank_tok) * HALF + tok_in
    for c in range(4):
        rows = lax.broadcasted_iota(jnp.int32, (128, CH), 0) + c * 128
        chooser[c * 128:(c + 1) * 128, :] = jnp.where(rows == target, 1.0, 0.0).astype(BF16)

    c_old.wait()
    pick_row = lax.broadcasted_iota(jnp.int32, (32, 256), 0)
    pick_col = lax.broadcasted_iota(jnp.int32, (32, 256), 1)
    wanted = (pick_row % 16) * 16 + 2 * g + pick_row // 16
    pick = jnp.where(pick_col == wanted, 1.0, 0.0).astype(BF16)
    for c in range(OLD // 16):
        both = dot(pick, oldbuf[c].reshape(256, HD)).astype(BF16)
        oldkv[0, c * 16:(c + 1) * 16, :] = both[:16]
        oldkv[1, c * 16:(c + 1) * 16, :] = both[16:]

    second_step(0)
    c_tab.wait()
    c_ctx.wait()
    col = lax.broadcasted_iota(jnp.int32, (ROWS, OLD + FRESH), 1)
    fresh = col - OLD
    within = fresh % (FRESH // 2)
    col_slot = jnp.where(col < OLD, col // PAGE, 16 + within // HALF)
    col_in = jnp.where(col < OLD, col % PAGE, (fresh // (FRESH // 2)) * HALF + within % HALF)
    where_pos = jnp.full((ROWS, OLD + FRESH), 1 << 20, jnp.int32)
    tab = tabv[...]
    for j in range(MAXP):
        where_pos = jnp.where(tab[:, j:j + 1] == col_slot, j * PAGE + col_in, where_pos)
    row_id = lax.broadcasted_iota(jnp.int32, (ROWS, 1), 0)
    lens = jnp.zeros((ROWS, 1), jnp.int32)
    for r in range(ROWS):
        lens = jnp.where(row_id == r, ctxs[r], lens)
    pos[...] = jnp.where(where_pos < lens, 0.0, NEG)

    def page_copy(c, i):
        dst = i + (SECT + i - s) // SECT
        return pltpu.make_async_remote_copy(
            src_ref=outg.at[c, pl.ds(pl.multiple_of(dst * MSG, MSG), MSG)],
            dst_ref=pool.at[k, c, pl.ds(pl.multiple_of(s * MSG, MSG), MSG)],
            send_sem=aa_s.at[c], recv_sem=aa_r.at[c], device_id=(dst, t), device_id_type=MESH,
        )

    def page_start(chunks, begin, end):
        def body(i, _):
            for c in chunks:
                page_copy(c, i).start()
            return 0
        lax.fori_loop(begin, end, body, 0)

    def pages_all(c):
        most = pl.ds(0, 31 * MSG)
        return pltpu.make_async_remote_copy(
            src_ref=outg.at[c, most], dst_ref=pool.at[k, c, most],
            send_sem=aa_s.at[c], recv_sem=aa_r.at[c], device_id=sib, device_id_type=MESH,
        )

    second_step(1)

    own = pl.ds(pl.multiple_of(s * MSG, MSG), MSG)
    for c in range(2):
        last_step(c)
        if c == 0:
            pl.semaphore_wait(flood.at[2], 2)
        for r in range(2):
            outg[c, r * 256:(r + 1) * 256] = dot(chooser[r * 256:(r + 1) * 256, :], kvc[c]).astype(BF16)
        if c == 0:
            page_start((0,), 0, EARLY)
        else:
            page_start((1,), 0, EARLY)
            page_start((0, 1), EARLY, 31)
        pool[k, c, own, :] = outg[c, own, :]
    halves = [kvc[c].astype(F32).reshape(TOK // PAGE, HALF, HD) for c in range(2)]
    kvh[k] = jnp.concatenate(halves, axis=1).reshape(TOK, HD).astype(BF16)
    c_kv = remote(kvh.at[k], kvh.at[k], sib_s.at[1], sib_r.at[1], sib)

    c_qp.wait()
    c_doc.wait()
    doc_row = docv[...].astype(F32)
    doc_col = jnp.broadcast_to(doc_row, (8, TOK)).T[:, 0:1]
    c_kv.wait_recv()
    out_copies = []
    for b in range(4):
        lo, hi = max(0, b - 2) * 128, (b + 1) * 128
        q0 = b * 128
        tq = lax.broadcasted_iota(jnp.int32, (128, hi - lo), 0) + q0
        tk = lax.broadcasted_iota(jnp.int32, (128, hi - lo), 1) + lo
        allowed = (doc_col[q0:hi, :] == doc_row[:, lo:hi]) & (tk <= tq)
        keys = kvh[0, lo:hi, :]
        values = kvh[1, lo:hi, :]
        for n in range(NH):
            sc = dot_t(qp[q0:hi, n * HD:(n + 1) * HD], keys) * SCALE
            wts = softmax_weights(jnp.where(allowed, sc, NEG))
            obuf[q0:hi, n * HD:(n + 1) * HD] = dot(wts, values).astype(BF16)
        out_copies.append(load(obuf.at[q0:hi], o_pre.at[q0:hi], out_sem.at[b]))

    c_qd.wait()
    qs = jnp.concatenate([qd[:, n * HD:(n + 1) * HD] for n in range(NH)], axis=0)
    mask = jnp.concatenate([pos[...]] * NH, axis=0)
    score = [dot_t(qs, oldkv[0]) * SCALE + mask[:, :OLD]]
    peak = jnp.max(score[0], axis=-1, keepdims=True)
    half = FRESH // 2
    c_pool = []
    for c in [c_st] + list(c_ps.values()) + sends:
        c.wait_send()
    for c in range(2):
        pages_all(c).wait_recv()
        c_pool.append(remote(pool.at[k, c], pool.at[k, c], sib_s.at[2 + c], sib_r.at[2 + c], sib))
    for c in range(2):
        c_pool[c].wait_recv()
        sc = dot_t(qs, pool[0, c]) * SCALE + mask[:, OLD + c * half:OLD + (c + 1) * half]
        score.append(sc)
        peak = jnp.maximum(peak, jnp.max(sc, axis=-1, keepdims=True))
    raised = [jnp.exp(sc - peak) for sc in score]
    norm = sum(jnp.sum(e, axis=-1, keepdims=True) for e in raised)
    norm = 1.0 / norm
    mixed = dot((raised[0] * norm).astype(BF16), oldkv[1])
    for c in range(2):
        mixed = mixed + dot((raised[1 + c] * norm).astype(BF16), pool[1, c])
    mixed = mixed.astype(BF16)
    for n in range(NH):
        o_dec[:, n * HD:(n + 1) * HD] = mixed[n * ROWS:(n + 1) * ROWS]

    for c in [c_kv] + c_pool:
        c.wait_send()
    for c in range(2):
        pages_all(c).wait_send()
    for c in out_copies:
        c.wait()


def local(hidden_pre, norm_gain, kv_weight, query_pre, doc_ids, page_dest, old_pages, query_dec, page_table, ctx_len):
    any_spec = pl.BlockSpec(memory_space=pl.ANY)
    dma = pltpu.SemaphoreType.DMA
    vm = pltpu.VMEM
    I32 = jnp.int32
    I16 = jnp.int16
    return pl.pallas_call(
        kernel,
        name="serve",
        out_shape=(
            jax.ShapeDtypeStruct((TOK, NH * HD), BF16),
            jax.ShapeDtypeStruct((ROWS, NH * HD), BF16),
        ),
        in_specs=[any_spec] * 10,
        out_specs=(any_spec, pl.BlockSpec(memory_space=vm)),
        scratch_shapes=[
            vm((TOK, FEAT), BF16), vm((FEAT,), BF16), vm((CHIPS, FEAT, 2 * HD), BF16),
            vm((1, TOK), I32), vm((1, 32), I32), vm((ROWS, MAXP), I32), pltpu.SMEM((ROWS,), I32),
            vm((TOK, FEAT), BF16), vm((2, 8, 128), F32),
            vm((CHIPS, 2, TOK, HD), F32), vm((CHIPS, TOK, HD), F32),
            vm((CHIPS, TOK, HD), I16), vm((2, 4, RH, HD), I16), vm((2, 14, RH, HD), I16),
            vm((12, 8, HD), F32), vm((12, 8, HD), F32), vm((TOK, HD), F32),
            vm((FRESH // 2, CH), BF16), vm((2, CH, HD), BF16), vm((2, FRESH // 2, HD), BF16),
            vm((2, TOK, HD), BF16), vm((2, 2, FRESH // 2, HD), BF16),
            vm((16, 16, 16, HD), BF16), vm((2, OLD, HD), BF16), vm((TOK, NH * HD), BF16),
            vm((ROWS, NH * HD), BF16), vm((ROWS, OLD + FRESH), F32),
            vm((TOK, NH * HD), BF16),
            dma((9,)), dma((8,)), dma((4,)), dma((4,)), dma((8,)), dma((8,)), dma((28,)), dma((28,)),
            dma((12,)), dma((12,)), dma((2,)), dma((2,)), dma((4,)), pltpu.SemaphoreType.REGULAR((3,)),
        ],
        compiler_params=pltpu.CompilerParams(
            collective_id=0, has_side_effects=True, vmem_limit_bytes=VMEM_LIMIT
        ),
    )(
        hidden_pre, norm_gain, kv_weight, query_pre, doc_ids, page_dest.reshape(1, 32), old_pages,
        query_dec, page_table, ctx_len,
    )


def solution(mesh):
    in_specs = (
        P("sect", "tp"),
        P("tp"),
        P("tp", None),
        P("sect", "tp"),
        P("sect", None),
        P("sect", None),
        P("sect", None, None, None),
        P("sect", "tp"),
        P("sect", None),
        P("sect"),
    )
    out_specs = (P("sect", "tp"), P("sect", "tp"))
    return jax.shard_map(local, mesh=mesh, in_specs=in_specs, out_specs=out_specs, check_vma=False)
```

```python
import jax
import jax.numpy as jnp
from jax import lax
from jax.sharding import PartitionSpec as P
import jax.experimental.pallas as pl
import jax.experimental.pallas.tpu as pltpu

D = 8192
HD = 128
PAGE = 16
TOK = 512
FEAT = 512
CHIPS = 8
SECT = 32
SLOTS = 2
HALF = PAGE // 2
CH = TOK // 2
MSG = SLOTS * HALF
FRESH = SECT * SLOTS * PAGE
LAG = 2
AHEAD = 2
EARLY = 10
RH = CH // 2
KEYS = ((1, 2), (0, 2), (1, 1), (0, 1), (1, 0), (1, 3), (0, 3), (0, 0))
ROWS = 16
NH = 4
OLD = 256
MAXP = 16
NORM_EPS = 1e-05
SCALE = HD ** -0.5
MESH = pl.DeviceIdType.MESH
F32 = jnp.float32
BF16 = jnp.bfloat16
NEG = -jnp.inf
TINY = 1e-30
STEPS = 32000.0
VMEM_LIMIT = 60 * 2**20


def dot(a, b):
    return lax.dot_general(a, b, (((1,), (0,)), ((), ())), preferred_element_type=F32)


def dot_t(a, b):
    return lax.dot_general(a, b, (((1,), (1,)), ((), ())), preferred_element_type=F32)


def softmax_weights(scores):
    peak = jnp.max(scores, axis=-1, keepdims=True)
    raised = jnp.exp(scores - peak)
    return (raised * (1.0 / jnp.sum(raised, axis=-1, keepdims=True))).astype(BF16)


def kernel(
    hid, gain, weight, qpre, doc, pdest, oldp, qdec, table, ctx,
    o_pre, o_dec,
    hraw, graw, wv, docv, pdv, tabv, ctxs, hs, st, part, sibp, sbuf, sbuf2, rs, nsend, nrecv, rowb, chooser, kvc, outg, kvh, pool,
    oldbuf, oldkv, qp, qd, pos, obuf,
    in_sem, w_sem, sib_s, sib_r, ps_s, ps_r, rs_s, rs_r, sq_s, sq_r, aa_s, aa_r, out_sem, flood,
):
    s = lax.axis_index("sect")
    t = lax.axis_index("tp")
    k = t % 2
    x = (t // 2) % 4
    yh = t // 8
    g = t // 2
    z = s // 2
    yl = s % 2
    sib = (s, t + 1 - 2 * k)

    def head(rel, dx):
        return ((yh + rel) % 2) * 4 + (x + dx) % 4

    def chip(rel, dx):
        return (s, head(rel, dx) * 2 + k)

    def z_peer(dz, yx):
        return (((z + dz + 16) % 16) * 2 + (yl + yx) % 2, t)

    def remote(src, dst, ss, rr, dev):
        c = pltpu.make_async_remote_copy(
            src_ref=src, dst_ref=dst, send_sem=ss, recv_sem=rr, device_id=dev, device_id_type=MESH
        )
        c.start()
        return c

    def load(src, dst, sem):
        c = pltpu.make_async_copy(src, dst, sem)
        c.start()
        return c

    bar = pltpu.get_barrier_semaphore()
    greeted = [sib, chip(1, 0), chip(0, 1), chip(0, 2), chip(0, 3)]
    greeted += [z_peer(1, 0), z_peer(-1, 0), z_peer(1, 1), z_peer(-1, 1), z_peer(0, 1)]
    for peer in greeted:
        pl.semaphore_signal(bar, inc=1, device_id=peer, device_id_type=MESH)

    c_hid = load(hid, hraw, in_sem.at[0])
    c_gain = load(gain, graw, in_sem.at[1])
    c_w = {}
    for n, key in enumerate(KEYS):
        j = head(*key)
        c_w[key] = load(
            weight.at[:, pl.ds(pl.multiple_of(j * 2 * HD, 2 * HD), 2 * HD)], wv.at[j], w_sem.at[n]
        )
    c_pd = load(pdest, pdv, in_sem.at[2])
    c_doc = load(doc, docv, in_sem.at[3])
    c_tab = load(table, tabv, in_sem.at[4])
    c_ctx = load(ctx, ctxs, in_sem.at[5])
    c_old = load(oldp, oldbuf, in_sem.at[6])
    c_qp = load(qpre, qp, in_sem.at[7])
    c_qd = load(qdec, qd, in_sem.at[8])

    c_hid.wait()
    c_gain.wait()
    h = hraw[...].astype(F32).reshape(TOK // PAGE, PAGE, FEAT)
    h = jnp.concatenate([h[:, :HALF].reshape(CH, FEAT), h[:, HALF:].reshape(CH, FEAT)], axis=0)
    hs[...] = (h * graw[...].astype(F32).reshape(1, FEAT)).astype(BF16)
    hh = h * h
    folded = hh[:, 0:128] + hh[:, 128:256] + hh[:, 256:384] + hh[:, 384:512]
    sq_row = jnp.sum(folded.T, axis=0, keepdims=True)
    for q in range(4):
        st[k, q:q + 1, :] = sq_row[:, q * 128:(q + 1) * 128]
    st[k, 4:8, :] = jnp.zeros((4, 128), F32)

    c_ps, sends, inbox, notes = {}, [], {}, {}
    nsend[...] = jnp.zeros(nsend.shape, F32)

    def signal_round(r):
        for sign in (1, -1):
            pl.semaphore_signal(
                flood.at[r], inc=1, device_id=z_peer(sign * (1 << r), 0), device_id_type=MESH
            )

    def norm_col(sq):
        return lax.rsqrt(sq * (1.0 / (2 * FEAT)) + TINY).T

    def scale_col(sq):
        ms = sq * (1.0 / (2 * FEAT)) + TINY
        return (ms * lax.rsqrt(ms)).T

    def spread(cols, quarter):
        return jnp.broadcast_to(cols[:, quarter:quarter + 1], (RH, HD))

    def code(level):
        top = jnp.maximum(jnp.max(jnp.abs(level), axis=0, keepdims=True), TINY)
        return jnp.round(level * (STEPS / top)).astype(jnp.int32).astype(jnp.int16), top * (1.0 / STEPS)

    def post(key, src, dst, index, peer):
        inbox[key] = remote(src, dst, rs_s.at[index], rs_r.at[index], peer)
        sends.append(inbox[key])

    def post_first(c, rel, dx):
        j = head(rel, dx)
        if rel == 1:
            post((c, "up", dx), sbuf.at[j, pl.ds(c * CH, RH)], rs.at[c, dx], c * 14 + dx, chip(1, 0))
        if dx > 0:
            slot = 4 + 2 * (dx - 1) + rel
            post(
                (c, "low", rel, dx), sbuf.at[j, pl.ds(c * CH + RH, RH)], rs.at[c, slot], c * 14 + slot,
                chip(0, dx),
            )

    def post_note(note, sq, lines, peer):
        nsend[note, 0:4, :] = sq[0:4]
        for line, value in lines:
            nsend[note, line:line + 1, :] = value
        notes[note] = remote(nsend.at[note], nrecv.at[note], sq_s.at[note], sq_r.at[note], peer)
        sends.append(notes[note])

    def decode(c, slot, stat, line):
        return rs[c, slot].astype(jnp.int32).astype(F32) * stat[line:line + 1, :]

    steps = {}
    done = 0
    for q in range(8 + LAG):
        if q < 8:
            j = head(*KEYS[q])
            c_w[KEYS[q]].wait()
            both = dot(hs[...], wv[j])
            part[j, 0] = both[:, :HD]
            part[j, 1] = both[:, HD:]
        if q < AHEAD - 1:
            continue
        if q == AHEAD - 1:
            pl.semaphore_wait(bar, len(greeted))
            c_st = remote(st.at[k], st.at[k], sib_s.at[0], sib_r.at[0], sib)
            signal_round(0)
        for p in range(q if q >= AHEAD else 0, q + 1):
            if p < 8:
                j = head(*KEYS[p])
                c_ps[p] = remote(part.at[j, 1 - k], sibp.at[j], ps_s.at[p], ps_r.at[p], sib)
        while done <= q - LAG:
            p = done
            done += 1
            if p == 0:
                c_st.wait_recv()
                chip_sq = st[0] + st[1]
                chip_col = norm_col(chip_sq)
                for quarter in range(4):
                    rowb[quarter * RH:(quarter + 1) * RH] = spread(chip_col, quarter)
            rel, dx = KEYS[p]
            j = head(rel, dx)
            c_ps[p].wait_recv()
            total = part[j, k] + sibp[j]
            part[j, k] = total
            if (rel, dx) == (0, 0):
                continue
            if p == 2:
                pl.semaphore_wait(flood.at[0], 2)
                signal_round(1)
            sbuf[j], steps[rel, dx] = code(total * rowb[...])
            post_first(0, rel, dx)
            if (rel, dx) == (1, 3):
                post_note(0, chip_sq, [(4 + n, steps[1, n]) for n in range(4)], chip(1, 0))
            if rel == 0:
                post_note(dx, chip_sq, [(4, steps[0, dx]), (5, steps[1, dx])], chip(0, dx))
    for rel, dx in KEYS:
        post_first(1, rel, dx)
    pl.semaphore_wait(flood.at[1], 2)
    signal_round(2)

    known = {}

    def second_step(c):
        if c == 0:
            notes[0].wait_recv()
            stat = nrecv[0]
            known["row_sq"] = chip_sq + stat
            known["row_col"] = norm_col(known["row_sq"])
            known["up"] = scale_col(stat)
        for dx in (2, 1, 3):
            inbox[c, "up", dx].wait_recv()
        scale = spread(known["up"], 2 * c)
        norm = spread(known["row_col"], 2 * c)
        lines = {}
        for dx in (2, 1, 3):
            value = decode(c, dx, nrecv[0], 4 + dx) * scale + part[head(0, dx), k, c * CH:c * CH + RH]
            sbuf2[c, dx - 1], lines[dx] = code(value * norm)
        for dx in (2, 1, 3):
            post((c, dx), sbuf2.at[c, dx - 1], rs.at[c, 9 + dx], c * 14 + 9 + dx, chip(0, dx))
            post_note(3 + 4 * c + dx, known["row_sq"], [(4, lines[dx])], chip(0, dx))
        if c == 0:
            quad_sq = chip_sq
            for dx in (2, 1, 3):
                notes[dx].wait_recv()
                stat = nrecv[dx]
                known[dx] = scale_col(stat)
                quad_sq = quad_sq + stat
            known["quad_sq"] = quad_sq
            known["quad_col"] = norm_col(quad_sq)
        for dx in (2, 1, 3):
            inbox[c, "low", 1, dx].wait_recv()
        value = part[head(1, 0), k, c * CH + RH:(c + 1) * CH]
        for dx in (2, 1, 3):
            value = value + decode(c, 5 + 2 * (dx - 1), nrecv[dx], 5) * spread(known[dx], 2 * c + 1)
        sbuf2[c, 3], line = code(value * spread(known["quad_col"], 2 * c + 1))
        post((c, 13), sbuf2.at[c, 3], rs.at[c, 13], c * 14 + 13, chip(1, 0))
        post_note(7 + 4 * c, known["quad_sq"], [(4, line)], chip(1, 0))

    def last_step(c):
        for dx in (1, 3, 2):
            notes[3 + 4 * c + dx].wait_recv()
        if c == 0:
            total_sq = known["row_sq"]
            for dx in (1, 3, 2):
                known[3 + dx] = scale_col(nrecv[3 + dx])
                total_sq = total_sq + nrecv[3 + dx]
            known["inv"] = lax.rsqrt(total_sq / D + NORM_EPS).T
        inbox[c, "up", 0].wait_recv()
        for dx in (1, 2, 3):
            inbox[c, "low", 0, dx].wait_recv()
            inbox[c, dx].wait_recv()
        notes[7 + 4 * c].wait_recv()
        inbox[c, 13].wait_recv()
        if c == 0:
            known[7] = scale_col(nrecv[7])
        top = decode(c, 0, nrecv[0], 4) * spread(known["up"], 2 * c) + part[g, k, c * CH:c * CH + RH]
        low = part[g, k, c * CH + RH:(c + 1) * CH]
        for dx in (1, 3, 2):
            top = top + decode(c, 9 + dx, nrecv[3 + 4 * c + dx], 4) * spread(known[3 + dx], 2 * c)
            low = low + decode(c, 4 + 2 * (dx - 1), nrecv[dx], 4) * spread(known[dx], 2 * c + 1)
        low = low + decode(c, 13, nrecv[7 + 4 * c], 4) * spread(known[7], 2 * c + 1)
        kvc[c, 0:RH] = (top * spread(known["inv"], 2 * c)).astype(BF16)
        kvc[c, RH:CH] = (low * spread(known["inv"], 2 * c + 1)).astype(BF16)

    c_pd.wait()
    eye = lax.broadcasted_iota(jnp.int32, (32, 32), 0) == lax.broadcasted_iota(jnp.int32, (32, 32), 1)
    page_col = jnp.sum(jnp.where(eye, jnp.broadcast_to(pdv[...], (32, 32)), 0), axis=1, keepdims=True)
    page_of = lax.broadcasted_iota(jnp.int32, (32, CH), 1) // HALF
    page_row = lax.broadcasted_iota(jnp.int32, (32, CH), 0)
    page_b = jnp.broadcast_to(page_col, (32, CH))
    dest_tok = jnp.sum(jnp.where(page_of == page_row, page_b, 0), axis=0, keepdims=True)
    rank_tok = jnp.sum(
        jnp.where((page_b == dest_tok) & (page_row < page_of), 1, 0), axis=0, keepdims=True
    )
    tok_in = lax.broadcasted_iota(jnp.int32, (1, CH), 1) % HALF
    target = (dest_tok * SLOTS + rank_tok) * HALF + tok_in
    for c in range(4):
        rows = lax.broadcasted_iota(jnp.int32, (128, CH), 0) + c * 128
        chooser[c * 128:(c + 1) * 128, :] = jnp.where(rows == target, 1.0, 0.0).astype(BF16)

    c_old.wait()
    pick_row = lax.broadcasted_iota(jnp.int32, (32, 256), 0)
    pick_col = lax.broadcasted_iota(jnp.int32, (32, 256), 1)
    wanted = (pick_row % 16) * 16 + 2 * g + pick_row // 16
    pick = jnp.where(pick_col == wanted, 1.0, 0.0).astype(BF16)
    for c in range(OLD // 16):
        both = dot(pick, oldbuf[c].reshape(256, HD)).astype(BF16)
        oldkv[0, c * 16:(c + 1) * 16, :] = both[:16]
        oldkv[1, c * 16:(c + 1) * 16, :] = both[16:]

    second_step(0)
    c_tab.wait()
    c_ctx.wait()
    col = lax.broadcasted_iota(jnp.int32, (ROWS, OLD + FRESH), 1)
    fresh = col - OLD
    within = fresh % (FRESH // 2)
    col_slot = jnp.where(col < OLD, col // PAGE, 16 + within // HALF)
    col_in = jnp.where(col < OLD, col % PAGE, (fresh // (FRESH // 2)) * HALF + within % HALF)
    where_pos = jnp.full((ROWS, OLD + FRESH), 1 << 20, jnp.int32)
    tab = tabv[...]
    for j in range(MAXP):
        where_pos = jnp.where(tab[:, j:j + 1] == col_slot, j * PAGE + col_in, where_pos)
    row_id = lax.broadcasted_iota(jnp.int32, (ROWS, 1), 0)
    lens = jnp.zeros((ROWS, 1), jnp.int32)
    for r in range(ROWS):
        lens = jnp.where(row_id == r, ctxs[r], lens)
    pos[...] = jnp.where(where_pos < lens, 0.0, NEG)

    def page_copy(c, i):
        dst = i + (SECT + i - s) // SECT
        return pltpu.make_async_remote_copy(
            src_ref=outg.at[c, pl.ds(pl.multiple_of(dst * MSG, MSG), MSG)],
            dst_ref=pool.at[k, c, pl.ds(pl.multiple_of(s * MSG, MSG), MSG)],
            send_sem=aa_s.at[c], recv_sem=aa_r.at[c], device_id=(dst, t), device_id_type=MESH,
        )

    def page_start(chunks, begin, end):
        def body(i, _):
            for c in chunks:
                page_copy(c, i).start()
            return 0
        lax.fori_loop(begin, end, body, 0)

    def pages_all(c):
        most = pl.ds(0, 31 * MSG)
        return pltpu.make_async_remote_copy(
            src_ref=outg.at[c, most], dst_ref=pool.at[k, c, most],
            send_sem=aa_s.at[c], recv_sem=aa_r.at[c], device_id=sib, device_id_type=MESH,
        )

    second_step(1)

    own = pl.ds(pl.multiple_of(s * MSG, MSG), MSG)
    for c in range(2):
        last_step(c)
        if c == 0:
            pl.semaphore_wait(flood.at[2], 2)
        for r in range(2):
            outg[c, r * 256:(r + 1) * 256] = dot(chooser[r * 256:(r + 1) * 256, :], kvc[c]).astype(BF16)
        if c == 0:
            page_start((0,), 0, EARLY)
        else:
            page_start((1,), 0, EARLY)
            page_start((0, 1), EARLY, 31)
        pool[k, c, own, :] = outg[c, own, :]
    halves = [kvc[c].astype(F32).reshape(TOK // PAGE, HALF, HD) for c in range(2)]
    kvh[k] = jnp.concatenate(halves, axis=1).reshape(TOK, HD).astype(BF16)
    c_kv = remote(kvh.at[k], kvh.at[k], sib_s.at[1], sib_r.at[1], sib)

    c_qp.wait()
    c_doc.wait()
    doc_row = docv[...].astype(F32)
    doc_col = jnp.broadcast_to(doc_row, (8, TOK)).T[:, 0:1]
    c_kv.wait_recv()
    out_copies = []
    for b in range(4):
        lo, hi = max(0, b - 2) * 128, (b + 1) * 128
        q0 = b * 128
        tq = lax.broadcasted_iota(jnp.int32, (128, hi - lo), 0) + q0
        tk = lax.broadcasted_iota(jnp.int32, (128, hi - lo), 1) + lo
        allowed = (doc_col[q0:hi, :] == doc_row[:, lo:hi]) & (tk <= tq)
        keys = kvh[0, lo:hi, :]
        values = kvh[1, lo:hi, :]
        for n in range(NH):
            sc = dot_t(qp[q0:hi, n * HD:(n + 1) * HD], keys) * SCALE
            wts = softmax_weights(jnp.where(allowed, sc, NEG))
            obuf[q0:hi, n * HD:(n + 1) * HD] = dot(wts, values).astype(BF16)
        out_copies.append(load(obuf.at[q0:hi], o_pre.at[q0:hi], out_sem.at[b]))

    c_qd.wait()
    qs = jnp.concatenate([qd[:, n * HD:(n + 1) * HD] for n in range(NH)], axis=0)
    mask = jnp.concatenate([pos[...]] * NH, axis=0)
    score = [dot_t(qs, oldkv[0]) * SCALE + mask[:, :OLD]]
    peak = jnp.max(score[0], axis=-1, keepdims=True)
    half = FRESH // 2
    c_pool = []
    for c in [c_st] + list(c_ps.values()) + sends:
        c.wait_send()
    for c in range(2):
        pages_all(c).wait_recv()
        c_pool.append(remote(pool.at[k, c], pool.at[k, c], sib_s.at[2 + c], sib_r.at[2 + c], sib))
        c_pool[c].wait_recv()
        sc = dot_t(qs, pool[0, c]) * SCALE + mask[:, OLD + c * half:OLD + (c + 1) * half]
        score.append(sc)
        peak = jnp.maximum(peak, jnp.max(sc, axis=-1, keepdims=True))
    raised = [jnp.exp(sc - peak) for sc in score]
    norm = sum(jnp.sum(e, axis=-1, keepdims=True) for e in raised)
    norm = 1.0 / norm
    mixed = dot((raised[0] * norm).astype(BF16), oldkv[1])
    for c in range(2):
        mixed = mixed + dot((raised[1 + c] * norm).astype(BF16), pool[1, c])
    mixed = mixed.astype(BF16)
    for n in range(NH):
        o_dec[:, n * HD:(n + 1) * HD] = mixed[n * ROWS:(n + 1) * ROWS]

    for c in [c_kv] + c_pool:
        c.wait_send()
    for c in range(2):
        pages_all(c).wait_send()
    for c in out_copies:
        c.wait()


def local(hidden_pre, norm_gain, kv_weight, query_pre, doc_ids, page_dest, old_pages, query_dec, page_table, ctx_len):
    any_spec = pl.BlockSpec(memory_space=pl.ANY)
    dma = pltpu.SemaphoreType.DMA
    vm = pltpu.VMEM
    I32 = jnp.int32
    I16 = jnp.int16
    return pl.pallas_call(
        kernel,
        name="serve",
        out_shape=(
            jax.ShapeDtypeStruct((TOK, NH * HD), BF16),
            jax.ShapeDtypeStruct((ROWS, NH * HD), BF16),
        ),
        in_specs=[any_spec] * 10,
        out_specs=(any_spec, pl.BlockSpec(memory_space=vm)),
        scratch_shapes=[
            vm((TOK, FEAT), BF16), vm((FEAT,), BF16), vm((CHIPS, FEAT, 2 * HD), BF16),
            vm((1, TOK), I32), vm((1, 32), I32), vm((ROWS, MAXP), I32), pltpu.SMEM((ROWS,), I32),
            vm((TOK, FEAT), BF16), vm((2, 8, 128), F32),
            vm((CHIPS, 2, TOK, HD), F32), vm((CHIPS, TOK, HD), F32),
            vm((CHIPS, TOK, HD), I16), vm((2, 4, RH, HD), I16), vm((2, 14, RH, HD), I16),
            vm((12, 8, HD), F32), vm((12, 8, HD), F32), vm((TOK, HD), F32),
            vm((FRESH // 2, CH), BF16), vm((2, CH, HD), BF16), vm((2, FRESH // 2, HD), BF16),
            vm((2, TOK, HD), BF16), vm((2, 2, FRESH // 2, HD), BF16),
            vm((16, 16, 16, HD), BF16), vm((2, OLD, HD), BF16), vm((TOK, NH * HD), BF16),
            vm((ROWS, NH * HD), BF16), vm((ROWS, OLD + FRESH), F32),
            vm((TOK, NH * HD), BF16),
            dma((9,)), dma((8,)), dma((4,)), dma((4,)), dma((8,)), dma((8,)), dma((28,)), dma((28,)),
            dma((12,)), dma((12,)), dma((2,)), dma((2,)), dma((4,)), pltpu.SemaphoreType.REGULAR((3,)),
        ],
        compiler_params=pltpu.CompilerParams(
            collective_id=0, has_side_effects=True, vmem_limit_bytes=VMEM_LIMIT
        ),
    )(
        hidden_pre, norm_gain, kv_weight, query_pre, doc_ids, page_dest.reshape(1, 32), old_pages,
        query_dec, page_table, ctx_len,
    )


def solution(mesh):
    in_specs = (
        P("sect", "tp"),
        P("tp"),
        P("tp", None),
        P("sect", "tp"),
        P("sect", None),
        P("sect", None),
        P("sect", None, None, None),
        P("sect", "tp"),
        P("sect", None),
        P("sect"),
    )
    out_specs = (P("sect", "tp"), P("sect", "tp"))
    return jax.shard_map(local, mesh=mesh, in_specs=in_specs, out_specs=out_specs, check_vma=False)
```

```python
import jax
import jax.numpy as jnp
from jax import lax
from jax.sharding import PartitionSpec as P
import jax.experimental.pallas as pl
import jax.experimental.pallas.tpu as pltpu

D = 8192
HD = 128
PAGE = 16
TOK = 512
FEAT = 512
CHIPS = 8
SECT = 32
SLOTS = 2
HALF = PAGE // 2
CH = TOK // 2
MSG = SLOTS * HALF
FRESH = SECT * SLOTS * PAGE
LAG = 2
AHEAD = 2
EARLY = 10
RH = CH // 2
KEYS = ((1, 2), (0, 2), (1, 1), (0, 1), (1, 0), (1, 3), (0, 3), (0, 0))
ROWS = 16
NH = 4
OLD = 256
MAXP = 16
NORM_EPS = 1e-05
SCALE = HD ** -0.5
MESH = pl.DeviceIdType.MESH
F32 = jnp.float32
BF16 = jnp.bfloat16
NEG = -jnp.inf
TINY = 1e-30
STEPS = 32000.0
VMEM_LIMIT = 60 * 2**20


def dot(a, b):
    return lax.dot_general(a, b, (((1,), (0,)), ((), ())), preferred_element_type=F32)


def dot_t(a, b):
    return lax.dot_general(a, b, (((1,), (1,)), ((), ())), preferred_element_type=F32)


def softmax_weights(scores):
    peak = jnp.max(scores, axis=-1, keepdims=True)
    raised = jnp.exp(scores - peak)
    return (raised * (1.0 / jnp.sum(raised, axis=-1, keepdims=True))).astype(BF16)


def kernel(
    hid, gain, weight, qpre, doc, pdest, oldp, qdec, table, ctx,
    o_pre, o_dec,
    hraw, graw, wv, docv, pdv, tabv, ctxs, hs, st, part, sibp, sbuf, sbuf2, rs, nsend, nrecv, rowb, chooser, kvc, outg, kvh, pool,
    oldbuf, oldkv, qp, qd, pos, obuf,
    in_sem, w_sem, sib_s, sib_r, ps_s, ps_r, rs_s, rs_r, sq_s, sq_r, aa_s, aa_r, out_sem, flood,
):
    s = lax.axis_index("sect")
    t = lax.axis_index("tp")
    k = t % 2
    x = (t // 2) % 4
    yh = t // 8
    g = t // 2
    z = s // 2
    yl = s % 2
    sib = (s, t + 1 - 2 * k)

    def head(rel, dx):
        return ((yh + rel) % 2) * 4 + (x + dx) % 4

    def chip(rel, dx):
        return (s, head(rel, dx) * 2 + k)

    def z_peer(dz, yx):
        return (((z + dz + 16) % 16) * 2 + (yl + yx) % 2, t)

    def remote(src, dst, ss, rr, dev):
        c = pltpu.make_async_remote_copy(
            src_ref=src, dst_ref=dst, send_sem=ss, recv_sem=rr, device_id=dev, device_id_type=MESH
        )
        c.start()
        return c

    def load(src, dst, sem):
        c = pltpu.make_async_copy(src, dst, sem)
        c.start()
        return c

    bar = pltpu.get_barrier_semaphore()
    greeted = [sib, chip(1, 0), chip(0, 1), chip(0, 2), chip(0, 3)]
    greeted += [z_peer(1, 0), z_peer(-1, 0), z_peer(1, 1), z_peer(-1, 1), z_peer(0, 1)]
    for peer in greeted:
        pl.semaphore_signal(bar, inc=1, device_id=peer, device_id_type=MESH)

    c_hid = load(hid, hraw, in_sem.at[0])
    c_gain = load(gain, graw, in_sem.at[1])
    c_w = {}
    for n, key in enumerate(KEYS):
        j = head(*key)
        c_w[key] = load(
            weight.at[:, pl.ds(pl.multiple_of(j * 2 * HD, 2 * HD), 2 * HD)], wv.at[j], w_sem.at[n]
        )
    c_pd = load(pdest, pdv, in_sem.at[2])
    c_doc = load(doc, docv, in_sem.at[3])
    c_tab = load(table, tabv, in_sem.at[4])
    c_ctx = load(ctx, ctxs, in_sem.at[5])
    c_old = load(oldp, oldbuf, in_sem.at[6])
    c_qp = load(qpre, qp, in_sem.at[7])
    c_qd = load(qdec, qd, in_sem.at[8])

    c_hid.wait()
    c_gain.wait()
    h = hraw[...].astype(F32).reshape(TOK // PAGE, PAGE, FEAT)
    h = jnp.concatenate([h[:, :HALF].reshape(CH, FEAT), h[:, HALF:].reshape(CH, FEAT)], axis=0)
    hs[...] = (h * graw[...].astype(F32).reshape(1, FEAT)).astype(BF16)
    hh = h * h
    folded = hh[:, 0:128] + hh[:, 128:256] + hh[:, 256:384] + hh[:, 384:512]
    sq_row = jnp.sum(folded.T, axis=0, keepdims=True)
    for q in range(4):
        st[k, q:q + 1, :] = sq_row[:, q * 128:(q + 1) * 128]
    st[k, 4:8, :] = jnp.zeros((4, 128), F32)

    c_ps, sends, inbox, notes = {}, [], {}, {}
    nsend[...] = jnp.zeros(nsend.shape, F32)

    def signal_round(r):
        for sign in (1, -1):
            pl.semaphore_signal(
                flood.at[r], inc=1, device_id=z_peer(sign * (1 << r), 0), device_id_type=MESH
            )

    def norm_col(sq):
        return lax.rsqrt(sq * (1.0 / (2 * FEAT)) + TINY).T

    def scale_col(sq):
        ms = sq * (1.0 / (2 * FEAT)) + TINY
        return (ms * lax.rsqrt(ms)).T

    def spread(cols, quarter):
        return jnp.broadcast_to(cols[:, quarter:quarter + 1], (RH, HD))

    def code(level):
        top = jnp.maximum(jnp.max(jnp.abs(level), axis=0, keepdims=True), TINY)
        return jnp.round(level * (STEPS / top)).astype(jnp.int32).astype(jnp.int16), top * (1.0 / STEPS)

    def post(key, src, dst, index, peer):
        inbox[key] = remote(src, dst, rs_s.at[index], rs_r.at[index], peer)
        sends.append(inbox[key])

    def post_first(c, rel, dx):
        j = head(rel, dx)
        if rel == 1:
            post((c, "up", dx), sbuf.at[j, pl.ds(c * CH, RH)], rs.at[c, dx], c * 14 + dx, chip(1, 0))
        if dx > 0:
            slot = 4 + 2 * (dx - 1) + rel
            post(
                (c, "low", rel, dx), sbuf.at[j, pl.ds(c * CH + RH, RH)], rs.at[c, slot], c * 14 + slot,
                chip(0, dx),
            )

    def post_note(note, sq, lines, peer):
        nsend[note, 0:4, :] = sq[0:4]
        for line, value in lines:
            nsend[note, line:line + 1, :] = value
        notes[note] = remote(nsend.at[note], nrecv.at[note], sq_s.at[note], sq_r.at[note], peer)
        sends.append(notes[note])

    def decode(c, slot, stat, line):
        return rs[c, slot].astype(jnp.int32).astype(F32) * stat[line:line + 1, :]

    steps = {}
    done = 0
    for q in range(8 + LAG):
        if q < 8:
            j = head(*KEYS[q])
            c_w[KEYS[q]].wait()
            both = dot(hs[...], wv[j])
            part[j, 0] = both[:, :HD]
            part[j, 1] = both[:, HD:]
        if q < AHEAD - 1:
            continue
        if q == AHEAD - 1:
            pl.semaphore_wait(bar, len(greeted))
            c_st = remote(st.at[k], st.at[k], sib_s.at[0], sib_r.at[0], sib)
            signal_round(0)
        for p in range(q if q >= AHEAD else 0, q + 1):
            if p < 8:
                j = head(*KEYS[p])
                c_ps[p] = remote(part.at[j, 1 - k], sibp.at[j], ps_s.at[p], ps_r.at[p], sib)
        while done <= q - LAG:
            p = done
            done += 1
            if p == 0:
                c_st.wait_recv()
                chip_sq = st[0] + st[1]
                chip_col = norm_col(chip_sq)
                for quarter in range(4):
                    rowb[quarter * RH:(quarter + 1) * RH] = spread(chip_col, quarter)
            rel, dx = KEYS[p]
            j = head(rel, dx)
            c_ps[p].wait_recv()
            total = part[j, k] + sibp[j]
            part[j, k] = total
            if (rel, dx) == (0, 0):
                continue
            if p == 2:
                pl.semaphore_wait(flood.at[0], 2)
                signal_round(1)
            sbuf[j], steps[rel, dx] = code(total * rowb[...])
            post_first(0, rel, dx)
            if (rel, dx) == (1, 3):
                post_note(0, chip_sq, [(4 + n, steps[1, n]) for n in range(4)], chip(1, 0))
            if rel == 0:
                post_note(dx, chip_sq, [(4, steps[0, dx]), (5, steps[1, dx])], chip(0, dx))
    for rel, dx in KEYS:
        post_first(1, rel, dx)
    pl.semaphore_wait(flood.at[1], 2)
    signal_round(2)

    known = {}

    def second_step(c):
        if c == 0:
            notes[0].wait_recv()
            stat = nrecv[0]
            known["row_sq"] = chip_sq + stat
            known["row_col"] = norm_col(known["row_sq"])
            known["up"] = scale_col(stat)
        for dx in (2, 1, 3):
            inbox[c, "up", dx].wait_recv()
        scale = spread(known["up"], 2 * c)
        norm = spread(known["row_col"], 2 * c)
        lines = {}
        for dx in (2, 1, 3):
            value = decode(c, dx, nrecv[0], 4 + dx) * scale + part[head(0, dx), k, c * CH:c * CH + RH]
            sbuf2[c, dx - 1], lines[dx] = code(value * norm)
        for dx in (2, 1, 3):
            post((c, dx), sbuf2.at[c, dx - 1], rs.at[c, 9 + dx], c * 14 + 9 + dx, chip(0, dx))
            post_note(3 + 4 * c + dx, known["row_sq"], [(4, lines[dx])], chip(0, dx))
        if c == 0:
            quad_sq = chip_sq
            for dx in (2, 1, 3):
                notes[dx].wait_recv()
                stat = nrecv[dx]
                known[dx] = scale_col(stat)
                quad_sq = quad_sq + stat
            known["quad_sq"] = quad_sq
            known["quad_col"] = norm_col(quad_sq)
        for dx in (2, 1, 3):
            inbox[c, "low", 1, dx].wait_recv()
        value = part[head(1, 0), k, c * CH + RH:(c + 1) * CH]
        for dx in (2, 1, 3):
            value = value + decode(c, 5 + 2 * (dx - 1), nrecv[dx], 5) * spread(known[dx], 2 * c + 1)
        sbuf2[c, 3], line = code(value * spread(known["quad_col"], 2 * c + 1))
        post((c, 13), sbuf2.at[c, 3], rs.at[c, 13], c * 14 + 13, chip(1, 0))
        post_note(7 + 4 * c, known["quad_sq"], [(4, line)], chip(1, 0))

    def last_step(c):
        for dx in (1, 3, 2):
            notes[3 + 4 * c + dx].wait_recv()
        if c == 0:
            total_sq = known["row_sq"]
            for dx in (1, 3, 2):
                known[3 + dx] = scale_col(nrecv[3 + dx])
                total_sq = total_sq + nrecv[3 + dx]
            known["inv"] = lax.rsqrt(total_sq / D + NORM_EPS).T
        inbox[c, "up", 0].wait_recv()
        for dx in (1, 2, 3):
            inbox[c, "low", 0, dx].wait_recv()
            inbox[c, dx].wait_recv()
        notes[7 + 4 * c].wait_recv()
        inbox[c, 13].wait_recv()
        if c == 0:
            known[7] = scale_col(nrecv[7])
        top = decode(c, 0, nrecv[0], 4) * spread(known["up"], 2 * c) + part[g, k, c * CH:c * CH + RH]
        low = part[g, k, c * CH + RH:(c + 1) * CH]
        for dx in (1, 3, 2):
            top = top + decode(c, 9 + dx, nrecv[3 + 4 * c + dx], 4) * spread(known[3 + dx], 2 * c)
            low = low + decode(c, 4 + 2 * (dx - 1), nrecv[dx], 4) * spread(known[dx], 2 * c + 1)
        low = low + decode(c, 13, nrecv[7 + 4 * c], 4) * spread(known[7], 2 * c + 1)
        kvc[c, 0:RH] = (top * spread(known["inv"], 2 * c)).astype(BF16)
        kvc[c, RH:CH] = (low * spread(known["inv"], 2 * c + 1)).astype(BF16)

    second_step(0)

    c_pd.wait()
    eye = lax.broadcasted_iota(jnp.int32, (32, 32), 0) == lax.broadcasted_iota(jnp.int32, (32, 32), 1)
    page_col = jnp.sum(jnp.where(eye, jnp.broadcast_to(pdv[...], (32, 32)), 0), axis=1, keepdims=True)
    page_of = lax.broadcasted_iota(jnp.int32, (32, CH), 1) // HALF
    page_row = lax.broadcasted_iota(jnp.int32, (32, CH), 0)
    page_b = jnp.broadcast_to(page_col, (32, CH))
    dest_tok = jnp.sum(jnp.where(page_of == page_row, page_b, 0), axis=0, keepdims=True)
    rank_tok = jnp.sum(
        jnp.where((page_b == dest_tok) & (page_row < page_of), 1, 0), axis=0, keepdims=True
    )
    tok_in = lax.broadcasted_iota(jnp.int32, (1, CH), 1) % HALF
    target = (dest_tok * SLOTS + rank_tok) * HALF + tok_in
    for c in range(4):
        rows = lax.broadcasted_iota(jnp.int32, (128, CH), 0) + c * 128
        chooser[c * 128:(c + 1) * 128, :] = jnp.where(rows == target, 1.0, 0.0).astype(BF16)

    def page_copy(c, i):
        dst = i + (SECT + i - s) // SECT
        return pltpu.make_async_remote_copy(
            src_ref=outg.at[c, pl.ds(pl.multiple_of(dst * MSG, MSG), MSG)],
            dst_ref=pool.at[k, c, pl.ds(pl.multiple_of(s * MSG, MSG), MSG)],
            send_sem=aa_s.at[c], recv_sem=aa_r.at[c], device_id=(dst, t), device_id_type=MESH,
        )

    def page_start(chunks, begin, end):
        def body(i, _):
            for c in chunks:
                page_copy(c, i).start()
            return 0
        lax.fori_loop(begin, end, body, 0)

    def pages_all(c):
        most = pl.ds(0, 31 * MSG)
        return pltpu.make_async_remote_copy(
            src_ref=outg.at[c, most], dst_ref=pool.at[k, c, most],
            send_sem=aa_s.at[c], recv_sem=aa_r.at[c], device_id=sib, device_id_type=MESH,
        )

    second_step(1)

    own = pl.ds(pl.multiple_of(s * MSG, MSG), MSG)
    for c in range(2):
        last_step(c)
        if c == 0:
            pl.semaphore_wait(flood.at[2], 2)
        for r in range(2):
            outg[c, r * 256:(r + 1) * 256] = dot(chooser[r * 256:(r + 1) * 256, :], kvc[c]).astype(BF16)
        if c == 0:
            page_start((0,), 0, EARLY)
        else:
            page_start((1,), 0, EARLY)
            page_start((0, 1), EARLY, 31)
        pool[k, c, own, :] = outg[c, own, :]
    halves = [kvc[c].astype(F32).reshape(TOK // PAGE, HALF, HD) for c in range(2)]
    kvh[k] = jnp.concatenate(halves, axis=1).reshape(TOK, HD).astype(BF16)
    c_kv = remote(kvh.at[k], kvh.at[k], sib_s.at[1], sib_r.at[1], sib)

    c_qp.wait()
    c_doc.wait()
    doc_row = docv[...].astype(F32)
    doc_col = jnp.broadcast_to(doc_row, (8, TOK)).T[:, 0:1]
    c_kv.wait_recv()
    out_copies = []
    for b in range(4):
        lo, hi = max(0, b - 2) * 128, (b + 1) * 128
        q0 = b * 128
        tq = lax.broadcasted_iota(jnp.int32, (128, hi - lo), 0) + q0
        tk = lax.broadcasted_iota(jnp.int32, (128, hi - lo), 1) + lo
        allowed = (doc_col[q0:hi, :] == doc_row[:, lo:hi]) & (tk <= tq)
        keys = kvh[0, lo:hi, :]
        values = kvh[1, lo:hi, :]
        for n in range(NH):
            sc = dot_t(qp[q0:hi, n * HD:(n + 1) * HD], keys) * SCALE
            wts = softmax_weights(jnp.where(allowed, sc, NEG))
            obuf[q0:hi, n * HD:(n + 1) * HD] = dot(wts, values).astype(BF16)
        out_copies.append(load(obuf.at[q0:hi], o_pre.at[q0:hi], out_sem.at[b]))

    c_old.wait()
    pick_row = lax.broadcasted_iota(jnp.int32, (32, 256), 0)
    pick_col = lax.broadcasted_iota(jnp.int32, (32, 256), 1)
    wanted = (pick_row % 16) * 16 + 2 * g + pick_row // 16
    pick = jnp.where(pick_col == wanted, 1.0, 0.0).astype(BF16)
    for c in range(OLD // 16):
        both = dot(pick, oldbuf[c].reshape(256, HD)).astype(BF16)
        oldkv[0, c * 16:(c + 1) * 16, :] = both[:16]
        oldkv[1, c * 16:(c + 1) * 16, :] = both[16:]

    c_tab.wait()
    c_ctx.wait()
    col = lax.broadcasted_iota(jnp.int32, (ROWS, OLD + FRESH), 1)
    fresh = col - OLD
    within = fresh % (FRESH // 2)
    col_slot = jnp.where(col < OLD, col // PAGE, 16 + within // HALF)
    col_in = jnp.where(col < OLD, col % PAGE, (fresh // (FRESH // 2)) * HALF + within % HALF)
    where_pos = jnp.full((ROWS, OLD + FRESH), 1 << 20, jnp.int32)
    tab = tabv[...]
    for j in range(MAXP):
        where_pos = jnp.where(tab[:, j:j + 1] == col_slot, j * PAGE + col_in, where_pos)
    row_id = lax.broadcasted_iota(jnp.int32, (ROWS, 1), 0)
    lens = jnp.zeros((ROWS, 1), jnp.int32)
    for r in range(ROWS):
        lens = jnp.where(row_id == r, ctxs[r], lens)
    pos[...] = jnp.where(where_pos < lens, 0.0, NEG)

    c_qd.wait()
    qs = jnp.concatenate([qd[:, n * HD:(n + 1) * HD] for n in range(NH)], axis=0)
    mask = jnp.concatenate([pos[...]] * NH, axis=0)
    score = [dot_t(qs, oldkv[0]) * SCALE + mask[:, :OLD]]
    peak = jnp.max(score[0], axis=-1, keepdims=True)
    half = FRESH // 2
    c_pool = []
    for c in [c_st] + list(c_ps.values()) + sends:
        c.wait_send()
    for c in range(2):
        pages_all(c).wait_recv()
        c_pool.append(remote(pool.at[k, c], pool.at[k, c], sib_s.at[2 + c], sib_r.at[2 + c], sib))
        c_pool[c].wait_recv()
        sc = dot_t(qs, pool[0, c]) * SCALE + mask[:, OLD + c * half:OLD + (c + 1) * half]
        score.append(sc)
        peak = jnp.maximum(peak, jnp.max(sc, axis=-1, keepdims=True))
    raised = [jnp.exp(sc - peak) for sc in score]
    norm = sum(jnp.sum(e, axis=-1, keepdims=True) for e in raised)
    norm = 1.0 / norm
    mixed = dot((raised[0] * norm).astype(BF16), oldkv[1])
    for c in range(2):
        mixed = mixed + dot((raised[1 + c] * norm).astype(BF16), pool[1, c])
    mixed = mixed.astype(BF16)
    for n in range(NH):
        o_dec[:, n * HD:(n + 1) * HD] = mixed[n * ROWS:(n + 1) * ROWS]

    for c in [c_kv] + c_pool:
        c.wait_send()
    for c in range(2):
        pages_all(c).wait_send()
    for c in out_copies:
        c.wait()


def local(hidden_pre, norm_gain, kv_weight, query_pre, doc_ids, page_dest, old_pages, query_dec, page_table, ctx_len):
    any_spec = pl.BlockSpec(memory_space=pl.ANY)
    dma = pltpu.SemaphoreType.DMA
    vm = pltpu.VMEM
    I32 = jnp.int32
    I16 = jnp.int16
    return pl.pallas_call(
        kernel,
        name="serve",
        out_shape=(
            jax.ShapeDtypeStruct((TOK, NH * HD), BF16),
            jax.ShapeDtypeStruct((ROWS, NH * HD), BF16),
        ),
        in_specs=[any_spec] * 10,
        out_specs=(any_spec, pl.BlockSpec(memory_space=vm)),
        scratch_shapes=[
            vm((TOK, FEAT), BF16), vm((FEAT,), BF16), vm((CHIPS, FEAT, 2 * HD), BF16),
            vm((1, TOK), I32), vm((1, 32), I32), vm((ROWS, MAXP), I32), pltpu.SMEM((ROWS,), I32),
            vm((TOK, FEAT), BF16), vm((2, 8, 128), F32),
            vm((CHIPS, 2, TOK, HD), F32), vm((CHIPS, TOK, HD), F32),
            vm((CHIPS, TOK, HD), I16), vm((2, 4, RH, HD), I16), vm((2, 14, RH, HD), I16),
            vm((12, 8, HD), F32), vm((12, 8, HD), F32), vm((TOK, HD), F32),
            vm((FRESH // 2, CH), BF16), vm((2, CH, HD), BF16), vm((2, FRESH // 2, HD), BF16),
            vm((2, TOK, HD), BF16), vm((2, 2, FRESH // 2, HD), BF16),
            vm((16, 16, 16, HD), BF16), vm((2, OLD, HD), BF16), vm((TOK, NH * HD), BF16),
            vm((ROWS, NH * HD), BF16), vm((ROWS, OLD + FRESH), F32),
            vm((TOK, NH * HD), BF16),
            dma((9,)), dma((8,)), dma((4,)), dma((4,)), dma((8,)), dma((8,)), dma((28,)), dma((28,)),
            dma((12,)), dma((12,)), dma((2,)), dma((2,)), dma((4,)), pltpu.SemaphoreType.REGULAR((3,)),
        ],
        compiler_params=pltpu.CompilerParams(
            collective_id=0, has_side_effects=True, vmem_limit_bytes=VMEM_LIMIT
        ),
    )(
        hidden_pre, norm_gain, kv_weight, query_pre, doc_ids, page_dest.reshape(1, 32), old_pages,
        query_dec, page_table, ctx_len,
    )


def solution(mesh):
    in_specs = (
        P("sect", "tp"),
        P("tp"),
        P("tp", None),
        P("sect", "tp"),
        P("sect", None),
        P("sect", None),
        P("sect", None, None, None),
        P("sect", "tp"),
        P("sect", None),
        P("sect"),
    )
    out_specs = (P("sect", "tp"), P("sect", "tp"))
    return jax.shard_map(local, mesh=mesh, in_specs=in_specs, out_specs=out_specs, check_vma=False)
```
